32 devices in a mesh: blk: 8 (over y, x, core), fsdp: 4 (over z).
Axes of the slice: x: 2, y: 2, z: 4, core: 2. Of those that a mesh axis runs over, the one named last changes fastest.
Arguments:
- decoder_states: bfloat16 [2048, 4096], P('blk', 'fsdp'), may hold values from -10 to 10
- w_query: bfloat16 [4096, 4096], P('blk', 'fsdp'), may hold values from -0.09375 to 0.09375
- w_out_t: bfloat16 [4096, 4096], P('blk', 'fsdp'), may hold values from -0.1875 to 0.1875
- enc_keys: bfloat16 [2048, 4096], P('blk', 'fsdp'), may hold values from -80 to 80
- enc_values: bfloat16 [2048, 4096], P('blk', 'fsdp'), may hold values from -6 to 6
Outputs:
- attended: bfloat16 [2048, 4096], P(('blk', 'fsdp'))
The draws below stay inside these ranges and needn't reach their ends.
All inputs are finite; a program needn't handle non-finite values.
Results may differ from the reference program's by a relative error of at most 0.0095.
Values may be sent and summed in bfloat16 or wider, within the bound.
No kernel may reach another device: no remote copies, remote signals or barrier semaphores. Data moves between devices by JAX's collectives and lax.ppermute only.
A program may use at most 128 MiB of HBM per device.

```python
import math
import jax
import jax.numpy as jnp
from jax import lax

D = 4096
HEADS = 64
HEAD_DIM = 64
HD = 4096
ROWS = 2048
ENC = 2048


def draw_decoder_states(key, part):
    subkeys = jax.random.split(jax.random.fold_in(key, 11), 1)
    result = jnp.clip(jax.random.normal(subkeys[0], (ROWS, D), jnp.float32), -6.0, 6.0)
    return result.astype(jnp.bfloat16)


def draw_enc_keys(key, part):
    subkeys = jax.random.split(jax.random.fold_in(key, 23), 1)
    width = HEADS * HEAD_DIM
    result = jnp.clip(2.0 * jax.random.normal(subkeys[0], (ENC, width), jnp.float32), -8.0, 8.0)
    return result.astype(jnp.bfloat16)


def levels(own_key, dims, cuts, smallest, top_value):
    gain = 1.0
    for axis_at, parts in cuts:
        heights = jax.random.uniform(jax.random.fold_in(jax.random.fold_in(own_key, 6), axis_at), (parts,), jnp.float32, smallest / len(cuts), top_value / len(cuts))
        gain = gain * jnp.repeat(jnp.exp(heights), dims[axis_at] // parts).reshape((-1,) + (1,) * (len(dims) - 1 - axis_at))
    return gain


def noise(key, dims, scale, bound, cuts=(), held_as=jnp.bfloat16):
    values = scale * jax.random.normal(key, dims, jnp.float32)
    if cuts:
        values = values * levels(key, dims, cuts, -0.22, 0.18)
    return jnp.clip(values, -bound, bound).astype(held_as)


def setup_inputs(seed: int = 0) -> dict:
    key_list = jax.random.split(jax.random.key(seed), 6)
    return {
        "decoder_states": draw_decoder_states(jax.random.fold_in(key_list[5], 71), 0),
        "w_query": noise(key_list[1], (D, HD), D ** -0.5, 0.09375, ((0, 8), (1, 4))),
        "w_out_t": noise(key_list[2], (D, HD), (HD // 4) ** -0.5, 0.1875, ((0, 8), (1, 4))),
        "enc_keys": draw_enc_keys(jax.random.fold_in(key_list[5], 71), 0),
        "enc_values": noise(key_list[4], (ENC, HD), 1.0, 6.0, ((0, 8), (1, 4))),
    }


def reference(decoder_states, w_query, w_out_t, enc_keys, enc_values):
    queries = jnp.dot(decoder_states, w_query, preferred_element_type=jnp.float32).astype(jnp.bfloat16)
    factor = 1.0 / math.sqrt(HEAD_DIM)

    def one_head(head_index):
        offset = (head_index * HEAD_DIM).astype(jnp.int32)
        query_head = lax.dynamic_slice_in_dim(queries, offset, HEAD_DIM, 1)
        key_head = lax.dynamic_slice_in_dim(enc_keys, offset, HEAD_DIM, 1)
        value_head = lax.dynamic_slice_in_dim(enc_values, offset, HEAD_DIM, 1)
        scores = lax.dot_general(query_head, key_head, (((1,), (1,)), ((), ())), preferred_element_type=jnp.float32) * factor
        row_top = lax.optimization_barrier(jnp.max(scores, axis=1, keepdims=True))
        weights = jnp.exp(scores - row_top)
        row_sum = lax.optimization_barrier(jnp.sum(weights, axis=1, keepdims=True))
        blended = jnp.dot(weights.astype(jnp.bfloat16), value_head, preferred_element_type=jnp.float32)
        return (blended / row_sum).astype(jnp.bfloat16)
    context = lax.map(one_head, jnp.arange(HEADS, dtype=jnp.int32))
    context = jnp.transpose(context, (1, 0, 2)).reshape(ROWS, HEADS * HEAD_DIM)
    return lax.dot_general(context, w_out_t, (((1,), (1,)), ((), ())), preferred_element_type=jnp.float32).astype(jnp.bfloat16)
```

```python
import math

import jax
import jax.numpy as jnp
from jax import lax
from jax.experimental import pallas as pl
from jax.experimental.pallas import tpu as pltpu
from jax.sharding import PartitionSpec as P

HEAD_DIM = 64
PAIR = 2 * HEAD_DIM
VMEM = 60 * 1024 * 1024


def absorb(fold_state, query_heads, key_rows, value_rows):
    running_top, running_sum, weighted = fold_state
    local_heads = query_heads.shape[1]
    key_heads = key_rows.reshape(key_rows.shape[0], local_heads, HEAD_DIM)
    value_heads = value_rows.reshape(value_rows.shape[0], local_heads, HEAD_DIM)
    scores = jnp.einsum(
        "qhd,khd->hqk", query_heads, key_heads, preferred_element_type=jnp.float32
    ) * (1.0 / math.sqrt(HEAD_DIM))
    new_top = jnp.max(scores, axis=2)
    rescale = jnp.exp(running_top - new_top)
    probability = jnp.exp(scores - new_top[:, :, None])
    running_sum = running_sum * rescale + jnp.sum(probability, axis=2)
    weighted = weighted * rescale[:, :, None] + jnp.einsum(
        "hqk,khd->hqd",
        probability.astype(jnp.bfloat16),
        value_heads,
        preferred_element_type=jnp.float32,
    )
    return (new_top, running_sum, weighted)


def gathered_shards(decoder_states, w_query, w_out_t, enc_keys, enc_values):
    query_full = lax.all_gather(w_query, "blk", axis=0, tiled=True)
    row_count = decoder_states.shape[0]
    columns = query_full.shape[1]
    local_heads = columns // HEAD_DIM
    queries = jnp.dot(
        lax.all_gather(decoder_states, "fsdp", axis=1, tiled=True),
        query_full,
        preferred_element_type=jnp.float32,
    ).astype(jnp.bfloat16)
    start_state = (
        jnp.full((local_heads, row_count), -jnp.inf, jnp.float32),
        jnp.zeros((local_heads, row_count), jnp.float32),
        jnp.zeros((local_heads, row_count, HEAD_DIM), jnp.float32),
    )
    query_heads = queries.reshape(row_count, local_heads, HEAD_DIM)
    final_state = absorb(
        start_state,
        query_heads,
        lax.all_gather(enc_keys, "blk", axis=0, tiled=True),
        lax.all_gather(enc_values, "blk", axis=0, tiled=True),
    )
    context = final_state[2] / final_state[1][:, :, None]
    context = jnp.transpose(context, (1, 0, 2)).reshape(row_count, columns).astype(jnp.bfloat16)
    out_full = lax.all_gather(w_out_t, "blk", axis=0, tiled=True)
    return lax.psum_scatter(
        lax.dot_general(
            context, out_full, (((1,), (1,)), ((), ())), preferred_element_type=jnp.float32
        ),
        "fsdp",
        scatter_dimension=0,
        tiled=True,
    ).astype(jnp.bfloat16)


CORE = [(b, b ^ 1) for b in range(8)]
ALONG_X = [(b, b ^ 2) for b in range(8)]
ALONG_Y = [(b, b ^ 4) for b in range(8)]


def z_partner(step):
    return [(z, z ^ step) for z in range(4)]


def over_core(a):
    return lax.ppermute(a, "blk", CORE)


def over_x(a):
    return lax.ppermute(a, "blk", ALONG_X)


def over_y(a):
    return lax.ppermute(a, "blk", ALONG_Y)


def after(value, *earlier):
    return lax.optimization_barrier((value,) + earlier)[0]


def relay(from_x, from_y):
    half = from_x.shape[0] // 2
    return over_x(from_y[:half]), over_y(from_x[half:])


def any_spec():
    return pl.BlockSpec(memory_space=pl.ANY)


def smem_spec():
    return pl.BlockSpec(memory_space=pltpu.SMEM)


def vmem_spec():
    return pl.BlockSpec(memory_space=pltpu.VMEM)


def project_queries(place, states, weights):
    rows, depth = states[0].shape
    columns = weights[0][3].shape[1]
    shard = depth // 2
    half = columns // 2
    count = len(states) + len(weights)

    def kernel(place_ref, *refs):
        state_refs = refs[: len(states)]
        weight_refs = refs[len(states) : count]
        mine_ref, other_ref, state_s, weight_s, total, sems = refs[count:]
        chip, core, plane = place_ref[0], place_ref[1], place_ref[2]
        state_copies, weight_copies = [], {}
        for step, ref in enumerate(state_refs):
            copy = pltpu.make_async_copy(ref, state_s.at[plane ^ step], sems.at[step])
            copy.start()
            state_copies.append(copy)
        for n, (ref, (chip_step, core_step, first, piece)) in enumerate(zip(weight_refs, weights)):
            begin = pl.multiple_of((core ^ core_step) * shard + first, 16)
            copy = pltpu.make_async_copy(
                ref,
                weight_s.at[chip ^ chip_step, pl.ds(begin, piece.shape[0])],
                sems.at[len(states) + n],
            )
            copy.start()
            weight_copies.setdefault(chip_step, []).append(copy)
        for copy in state_copies:
            copy.wait()
        for chip_step in range(4):
            for copy in weight_copies[chip_step]:
                copy.wait()
            part = jnp.dot(
                state_s[chip ^ chip_step],
                weight_s[chip ^ chip_step],
                preferred_element_type=jnp.float32,
            )
            total[...] = part if chip_step == 0 else total[...] + part
        factor = 1.0 / math.sqrt(HEAD_DIM)
        for ref, which in ((mine_ref, core), (other_ref, 1 - core)):
            begin = pl.multiple_of(which * half, half)
            queries = total[:, pl.ds(begin, half)].astype(jnp.bfloat16)
            ref[...] = (queries.astype(jnp.float32) * factor).astype(jnp.bfloat16)

    shape = jax.ShapeDtypeStruct((rows, half), jnp.bfloat16)
    return pl.pallas_call(
        kernel,
        out_shape=(shape, shape),
        in_specs=[smem_spec()] + [any_spec()] * count,
        out_specs=(vmem_spec(), vmem_spec()),
        scratch_shapes=[
            pltpu.VMEM((4, rows, depth), jnp.bfloat16),
            pltpu.VMEM((4, depth, columns), jnp.bfloat16),
            pltpu.VMEM((rows, columns), jnp.float32),
            pltpu.SemaphoreType.DMA((count,)),
        ],
        compiler_params=pltpu.CompilerParams(vmem_limit_bytes=VMEM),
        cost_estimate=pl.CostEstimate(
            flops=2 * rows * 4 * depth * columns,
            bytes_accessed=2 * 4 * depth * (rows + columns),
            transcendentals=0,
        ),
        name="project_queries",
    )(place, *states, *[w[3] for w in weights])


def pair_part(queries, keys, values):
    rows = queries.shape[0]
    first = lax.broadcasted_iota(jnp.int32, (rows, PAIR), 1) < HEAD_DIM
    found = []
    for head in range(2):
        masked = jnp.where(first if head == 0 else jnp.logical_not(first), queries, 0)
        scores = [
            lax.dot_general(
                masked, k, (((1,), (1,)), ((), ())), preferred_element_type=jnp.float32
            )
            for k in keys
        ]
        top = scores[0].max(axis=1, keepdims=True)
        for s in scores[1:]:
            top = jnp.maximum(top, s.max(axis=1, keepdims=True))
        both = None
        for s, v in zip(scores, values):
            probability = jnp.exp(s - top).astype(jnp.bfloat16)
            part = jnp.dot(probability, v, preferred_element_type=jnp.float32)
            both = part if both is None else both + part
        found.append((both[:, :PAIR], both[:, PAIR:], jnp.broadcast_to(top, (rows, PAIR))))
    return [jnp.where(first, a, b) for a, b in zip(*found)]


def attend(query_blocks, keys, values, before=None):
    rows, columns = query_blocks[0].shape
    pairs = columns // PAIR
    blocks = len(query_blocks)
    last = before is not None
    held = [] if before is None else [a for block in before for a in block]
    outs = blocks if last else 3 * blocks

    def kernel(*refs):
        refs = list(refs)
        q_refs = [refs.pop(0) for _ in range(blocks)]
        k_refs = [refs.pop(0) for _ in keys]
        v_refs = [refs.pop(0) for _ in values]
        held_refs = [refs.pop(0) for _ in held]
        out_refs = [refs.pop(0) for _ in range(outs)]
        ks = [r[...] for r in k_refs]
        vs = [
            jnp.concatenate([r[...], jnp.ones(r.shape, jnp.bfloat16)], axis=1) for r in v_refs
        ]
        for n in range(blocks):
            weighted, sums, tops = pair_part(q_refs[n][...], ks, vs)
            if last:
                weighted_0, sums_0, tops_0 = (r[...] for r in held_refs[3 * n : 3 * n + 3])
                top = jnp.maximum(tops, tops_0)
                now, then = jnp.exp(tops - top), jnp.exp(tops_0 - top)
                weighted = weighted * now + weighted_0 * then
                sums = sums * now + sums_0 * then
                out_refs[n][...] = (weighted / sums).astype(jnp.bfloat16)
            else:
                for ref, a in zip(out_refs[3 * n : 3 * n + 3], (weighted, sums, tops)):
                    ref[...] = a

    def spec(a):
        return pl.BlockSpec((a.shape[0], PAIR), lambda p: (0, p))

    args = list(query_blocks) + list(keys) + list(values) + held
    out_shape = [
        jax.ShapeDtypeStruct((rows, columns), jnp.bfloat16 if last else jnp.float32)
    ] * outs
    total_keys = sum(k.shape[0] for k in keys)
    found = pl.pallas_call(
        kernel,
        grid=(pairs,),
        out_shape=out_shape,
        in_specs=[spec(a) for a in args],
        out_specs=[spec(a) for a in out_shape],
        compiler_params=pltpu.CompilerParams(vmem_limit_bytes=VMEM),
        cost_estimate=pl.CostEstimate(
            flops=2 * 2 * blocks * rows * total_keys * columns * 4,
            bytes_accessed=sum(a.size * a.dtype.itemsize for a in args),
            transcendentals=blocks * rows * total_keys * (columns // HEAD_DIM),
        ),
        name="attend_last" if last else "attend_first",
    )(*args)
    if last:
        return found
    return [found[3 * n : 3 * n + 3] for n in range(blocks)]


def project_out(place, mine, other, weights):
    rows, half = mine.shape
    quarter = rows // 4
    width = sum(w.shape[0] for w in weights)

    def kernel(place_ref, mine_ref, other_ref, *refs):
        weight_refs = refs[: len(weights)]
        outs = refs[len(weights) : len(weights) + 4]
        context = refs[-1]
        core, plane = place_ref[1], place_ref[2]
        for step in range(4):
            begin = pl.multiple_of((plane ^ step) * quarter, quarter)
            here = slice(step * quarter, (step + 1) * quarter)
            for ref, which in ((mine_ref, core), (other_ref, 1 - core)):
                lanes = pl.ds(pl.multiple_of(which * half, half), half)
                context[here, lanes] = ref[pl.ds(begin, quarter), :]
        at = 0
        for ref in weight_refs:
            part = lax.dot_general(
                context[...],
                ref[...],
                (((1,), (1,)), ((), ())),
                preferred_element_type=jnp.float32,
            )
            for step in range(4):
                outs[step][:, at : at + ref.shape[0]] = part[
                    step * quarter : (step + 1) * quarter
                ].astype(outs[step].dtype)
            at += ref.shape[0]

    return pl.pallas_call(
        kernel,
        out_shape=[
            jax.ShapeDtypeStruct((quarter, width), jnp.float32 if step == 0 else jnp.bfloat16)
            for step in range(4)
        ],
        in_specs=[smem_spec()] + [vmem_spec()] * (2 + len(weights)),
        out_specs=[vmem_spec()] * 4,
        scratch_shapes=[pltpu.VMEM((rows, 2 * half), jnp.bfloat16)],
        compiler_params=pltpu.CompilerParams(vmem_limit_bytes=VMEM),
        cost_estimate=pl.CostEstimate(
            flops=2 * rows * 2 * half * width,
            bytes_accessed=2 * width * 2 * half,
            transcendentals=0,
        ),
        name="project_out",
    )(place, mine, other, *weights)


def add_up(place, groups, shard):
    rows = groups[0][1].shape[0]

    def kernel(place_ref, *refs):
        out_ref = refs[-1]
        chip, core = place_ref[0], place_ref[1]
        for n, (spots, *_) in enumerate(groups):
            own, *received = refs[4 * n : 4 * n + 4]
            at = 0
            for chip_step, core_step, first, size in spots:
                total = own[:, at : at + size]
                for ref in received:
                    total = total + ref[:, at : at + size].astype(jnp.float32)
                begin = ((chip ^ chip_step) * 2 + (core ^ core_step)) * shard + first
                out_ref[:, pl.ds(pl.multiple_of(begin, 128), size)] = total.astype(jnp.bfloat16)
                at += size

    args = [a for group in groups for a in group[1:]]
    return pl.pallas_call(
        kernel,
        out_shape=jax.ShapeDtypeStruct((rows, 8 * shard), jnp.bfloat16),
        in_specs=[smem_spec()] + [vmem_spec()] * len(args),
        out_specs=vmem_spec(),
        compiler_params=pltpu.CompilerParams(vmem_limit_bytes=VMEM),
        cost_estimate=pl.CostEstimate(
            flops=4 * rows * 8 * shard, bytes_accessed=12 * rows * 8 * shard, transcendentals=0
        ),
        name="add_up",
    )(place, *args)


def plane_shards(decoder_states, w_query, w_out_t, enc_keys, enc_values):
    block, plane = lax.axis_index("blk"), lax.axis_index("fsdp")
    chip, core = block // 2, block % 2
    place = jnp.stack([chip, core, plane]).astype(jnp.int32)
    shard = w_query.shape[0]
    half_shard = shard // 2
    half = enc_keys.shape[1] // 2

    states = [decoder_states] + [
        lax.ppermute(decoder_states, "fsdp", z_partner(step)) for step in (1, 2, 3)
    ]
    query_x, query_y = over_x(w_query), over_y(w_query)

    def columns(a, which):
        return lax.dynamic_slice_in_dim(a, which * half, half, 1)

    swapped = over_core(
        jnp.concatenate([columns(enc_keys, 1 - core), columns(enc_values, 1 - core)], axis=0)
    )
    row_count = enc_keys.shape[0]
    keys = jnp.concatenate([columns(enc_keys, core), swapped[:row_count]], axis=0)
    values = jnp.concatenate([columns(enc_values, core), swapped[row_count:]], axis=0)
    keys_x, keys_y = over_x(keys), over_y(keys)

    query_top, query_bottom = relay(query_x, query_y)
    values = after(values, query_x, query_y)
    values_x, values_y = over_x(values), over_y(values)
    keys_top, keys_bottom = relay(keys_x, keys_y)
    values_top, values_bottom = relay(values_x, values_y)

    out_own = after(w_out_t, keys_x, keys_y)
    out_x, out_y = over_x(out_own), over_y(out_own)
    out_top, out_bottom = relay(out_x, out_y)

    def with_sibling(chip_step, first, piece):
        return [(chip_step, 0, first, piece), (chip_step, 1, first, over_core(piece))]

    query_pieces = (
        with_sibling(0, 0, w_query)
        + with_sibling(1, 0, query_x)
        + with_sibling(2, 0, query_y)
        + with_sibling(3, 0, query_top)
        + with_sibling(3, half_shard, query_bottom)
    )
    out_groups = [
        with_sibling(0, 0, w_out_t),
        with_sibling(1, 0, out_x) + with_sibling(2, 0, out_y),
        with_sibling(3, 0, out_top) + with_sibling(3, half_shard, out_bottom),
    ]

    queries, queries_other = project_queries(place, states, query_pieces)
    query_blocks = [queries, over_core(queries_other)]
    before = attend(query_blocks, [keys, keys_x, keys_y], [values, values_x, values_y])
    context, context_other = attend(
        query_blocks, [keys_top, keys_bottom], [values_top, values_bottom], before
    )
    context_back = over_core(context_other)

    sums = []
    for group in out_groups:
        own, *sent = project_out(place, context, context_back, [piece for *_, piece in group])
        received = [
            lax.ppermute(part, "fsdp", z_partner(step + 1)) for step, part in enumerate(sent)
        ]
        spots = [(a, b, first, piece.shape[0]) for a, b, first, piece in group]
        sums.append((spots, own, *received))
    return add_up(place, sums, shard)


def solution(mesh):
    in_specs = (
        P("blk", "fsdp"),
        P("blk", "fsdp"),
        P("blk", "fsdp"),
        P("blk", "fsdp"),
        P("blk", "fsdp"),
    )
    out_specs = P(("blk", "fsdp"), None)
    by_planes = mesh.shape["blk"] == 8 and mesh.shape["fsdp"] == 4
    return jax.shard_map(
        plane_shards if by_planes else gathered_shards,
        mesh=mesh,
        in_specs=in_specs,
        out_specs=out_specs,
        check_vma=False,
    )
```

```python
import math

import jax
import jax.numpy as jnp
from jax import lax
from jax.experimental import pallas as pl
from jax.experimental.pallas import tpu as pltpu
from jax.sharding import PartitionSpec as P

HEAD_DIM = 64
PAIR = 2 * HEAD_DIM
VMEM = 60 * 1024 * 1024


def absorb(fold_state, query_heads, key_rows, value_rows):
    running_top, running_sum, weighted = fold_state
    local_heads = query_heads.shape[1]
    key_heads = key_rows.reshape(key_rows.shape[0], local_heads, HEAD_DIM)
    value_heads = value_rows.reshape(value_rows.shape[0], local_heads, HEAD_DIM)
    scores = jnp.einsum(
        "qhd,khd->hqk", query_heads, key_heads, preferred_element_type=jnp.float32
    ) * (1.0 / math.sqrt(HEAD_DIM))
    new_top = jnp.max(scores, axis=2)
    rescale = jnp.exp(running_top - new_top)
    probability = jnp.exp(scores - new_top[:, :, None])
    running_sum = running_sum * rescale + jnp.sum(probability, axis=2)
    weighted = weighted * rescale[:, :, None] + jnp.einsum(
        "hqk,khd->hqd",
        probability.astype(jnp.bfloat16),
        value_heads,
        preferred_element_type=jnp.float32,
    )
    return (new_top, running_sum, weighted)


def gathered_shards(decoder_states, w_query, w_out_t, enc_keys, enc_values):
    query_full = lax.all_gather(w_query, "blk", axis=0, tiled=True)
    row_count = decoder_states.shape[0]
    columns = query_full.shape[1]
    local_heads = columns // HEAD_DIM
    queries = jnp.dot(
        lax.all_gather(decoder_states, "fsdp", axis=1, tiled=True),
        query_full,
        preferred_element_type=jnp.float32,
    ).astype(jnp.bfloat16)
    start_state = (
        jnp.full((local_heads, row_count), -jnp.inf, jnp.float32),
        jnp.zeros((local_heads, row_count), jnp.float32),
        jnp.zeros((local_heads, row_count, HEAD_DIM), jnp.float32),
    )
    query_heads = queries.reshape(row_count, local_heads, HEAD_DIM)
    final_state = absorb(
        start_state,
        query_heads,
        lax.all_gather(enc_keys, "blk", axis=0, tiled=True),
        lax.all_gather(enc_values, "blk", axis=0, tiled=True),
    )
    context = final_state[2] / final_state[1][:, :, None]
    context = jnp.transpose(context, (1, 0, 2)).reshape(row_count, columns).astype(jnp.bfloat16)
    out_full = lax.all_gather(w_out_t, "blk", axis=0, tiled=True)
    return lax.psum_scatter(
        lax.dot_general(
            context, out_full, (((1,), (1,)), ((), ())), preferred_element_type=jnp.float32
        ),
        "fsdp",
        scatter_dimension=0,
        tiled=True,
    ).astype(jnp.bfloat16)


CORE = [(b, b ^ 1) for b in range(8)]
CROSS = [(b, b ^ (2 if b % 2 == 0 else 4)) for b in range(8)]
CROSS_BACK = [(b, b ^ (4 if b % 2 == 0 else 2)) for b in range(8)]

def over_core(a):
    return lax.ppermute(a, "blk", CORE)


def cross(a):
    return lax.ppermute(a, "blk", CROSS)


def cross_back(a):
    return lax.ppermute(a, "blk", CROSS_BACK)


def over_z(a, step):
    return lax.ppermute(a, "fsdp", [(z, z ^ step) for z in range(4)])


def after(value, *earlier):
    return lax.optimization_barrier((value,) + earlier)[0]


OWN, OWN_SWAPPED = (0, 0, 0), (0, 0, 1)
NEAR, NEAR_SWAPPED = (1, 2, 0), (2, 1, 1)
SIDE, SIDE_SWAPPED = (2, 1, 0), (1, 2, 1)
FAR, FAR_SWAPPED = (3, 3, 0), (3, 3, 1)


def owner(place_ref, whose):
    chip, core = place_ref[0], place_ref[1]
    even, odd, core_step = whose
    return chip ^ (even + core * (odd - even)), core ^ core_step


def any_spec():
    return pl.BlockSpec(memory_space=pl.ANY)


def smem_spec():
    return pl.BlockSpec(memory_space=pltpu.SMEM)


def vmem_spec():
    return pl.BlockSpec(memory_space=pltpu.VMEM)


def project_queries(place, states, weights):
    rows, depth = states[0].shape
    shard, columns = weights[0][1].shape
    half = columns // 2
    count = len(states) + len(weights)

    def kernel(place_ref, *refs):
        state_refs = refs[: len(states)]
        weight_refs = refs[len(states) : count]
        mine_ref, other_ref, state_s, weight_s, total, sems = refs[count:]
        core, plane = place_ref[1], place_ref[2]
        state_copies, weight_copies = [], []
        for n, ref in enumerate(state_refs):
            copy = pltpu.make_async_copy(ref, state_s.at[plane ^ n], sems.at[n])
            copy.start()
            state_copies.append(copy)
        for n, (ref, (whose, _)) in enumerate(zip(weight_refs, weights)):
            chip_at, core_at = owner(place_ref, whose)
            begin = pl.multiple_of(core_at * shard, shard)
            copy = pltpu.make_async_copy(
                ref, weight_s.at[chip_at, pl.ds(begin, shard)], sems.at[len(states) + n]
            )
            copy.start()
            weight_copies.append(copy)
        for copy in state_copies:
            copy.wait()
        for n, (whose, _) in enumerate(weights):
            weight_copies[n].wait()
            chip_at, core_at = owner(place_ref, whose)
            begin = pl.multiple_of(core_at * shard, shard)
            part = jnp.dot(
                state_s[chip_at, :, pl.ds(begin, shard)],
                weight_s[chip_at, pl.ds(begin, shard)],
                preferred_element_type=jnp.float32,
            )
            total[...] = part if n == 0 else total[...] + part
        factor = 1.0 / math.sqrt(HEAD_DIM)
        for ref, which in ((mine_ref, core), (other_ref, 1 - core)):
            begin = pl.multiple_of(which * half, half)
            queries = total[:, pl.ds(begin, half)].astype(jnp.bfloat16)
            ref[...] = (queries.astype(jnp.float32) * factor).astype(jnp.bfloat16)

    shape = jax.ShapeDtypeStruct((rows, half), jnp.bfloat16)
    return pl.pallas_call(
        kernel,
        out_shape=(shape, shape),
        in_specs=[smem_spec()] + [any_spec()] * count,
        out_specs=(vmem_spec(), vmem_spec()),
        scratch_shapes=[
            pltpu.VMEM((4, rows, depth), jnp.bfloat16),
            pltpu.VMEM((4, depth, columns), jnp.bfloat16),
            pltpu.VMEM((rows, columns), jnp.float32),
            pltpu.SemaphoreType.DMA((count,)),
        ],
        compiler_params=pltpu.CompilerParams(vmem_limit_bytes=VMEM),
        cost_estimate=pl.CostEstimate(
            flops=2 * rows * 4 * depth * columns,
            bytes_accessed=2 * 4 * depth * (rows + columns),
            transcendentals=0,
        ),
        name="project_queries",
    )(place, *states, *[w[1] for w in weights])


def pair_part(queries, keys, values):
    rows = queries.shape[0]
    first = lax.broadcasted_iota(jnp.int32, (rows, PAIR), 1) < HEAD_DIM
    found = []
    for head in range(2):
        masked = jnp.where(first if head == 0 else jnp.logical_not(first), queries, 0)
        scores = [
            lax.dot_general(
                masked, k, (((1,), (1,)), ((), ())), preferred_element_type=jnp.float32
            )
            for k in keys
        ]
        top = scores[0].max(axis=1, keepdims=True)
        for s in scores[1:]:
            top = jnp.maximum(top, s.max(axis=1, keepdims=True))
        both = None
        for s, v in zip(scores, values):
            probability = jnp.exp(s - top).astype(jnp.bfloat16)
            part = jnp.dot(probability, v, preferred_element_type=jnp.float32)
            both = part if both is None else both + part
        found.append((both[:, :PAIR], both[:, PAIR:], jnp.broadcast_to(top, (rows, PAIR))))
    return [jnp.where(first, a, b) for a, b in zip(*found)]


def attend(query_blocks, pieces, before=None):
    rows, columns = query_blocks[0].shape
    pairs = columns // PAIR
    blocks = len(query_blocks)
    last = before is not None
    held = [] if before is None else [a for block in before for a in block]
    outs = blocks if last else 3 * blocks

    def kernel(*refs):
        refs = list(refs)
        q_refs = [refs.pop(0) for _ in range(blocks)]
        k_refs = [refs.pop(0) for _ in pieces]
        v_refs = [refs.pop(0) for _ in pieces]
        held_refs = [refs.pop(0) for _ in held]
        out_refs = [refs.pop(0) for _ in range(outs)]
        ks = [r[...] for r in k_refs]
        vs = [
            jnp.concatenate([r[...], jnp.ones(r.shape, jnp.bfloat16)], axis=1) for r in v_refs
        ]
        for n in range(blocks):
            weighted, sums, tops = pair_part(q_refs[n][...], ks, vs)
            if last:
                weighted_0, sums_0, tops_0 = (r[...] for r in held_refs[3 * n : 3 * n + 3])
                top = jnp.maximum(tops, tops_0)
                now, then = jnp.exp(tops - top), jnp.exp(tops_0 - top)
                weighted = weighted * now + weighted_0 * then
                sums = sums * now + sums_0 * then
                out_refs[n][...] = (weighted / sums).astype(jnp.bfloat16)
            else:
                for ref, a in zip(out_refs[3 * n : 3 * n + 3], (weighted, sums, tops)):
                    ref[...] = a

    def spec(a, skip=0):
        return pl.BlockSpec((a.shape[0], PAIR), lambda p: (0, p + skip))

    args = list(query_blocks) + list(pieces) + list(pieces) + held
    in_specs = (
        [spec(a) for a in query_blocks]
        + [spec(a) for a in pieces]
        + [spec(a, pairs) for a in pieces]
        + [spec(a) for a in held]
    )
    out_shape = [
        jax.ShapeDtypeStruct((rows, columns), jnp.bfloat16 if last else jnp.float32)
    ] * outs
    total_keys = sum(a.shape[0] for a in pieces)
    found = pl.pallas_call(
        kernel,
        grid=(pairs,),
        out_shape=out_shape,
        in_specs=in_specs,
        out_specs=[spec(a) for a in out_shape],
        compiler_params=pltpu.CompilerParams(vmem_limit_bytes=VMEM),
        cost_estimate=pl.CostEstimate(
            flops=2 * 2 * blocks * rows * total_keys * columns * 4,
            bytes_accessed=sum(a.size * a.dtype.itemsize for a in args),
            transcendentals=blocks * rows * total_keys * (columns // HEAD_DIM),
        ),
        name="attend_last" if last else "attend_first",
    )(*args)
    if last:
        return found
    return [found[3 * n : 3 * n + 3] for n in range(blocks)]


def project_out(place, mine, other, weights, tiles=2):
    rows, half = mine.shape
    quarter = rows // 4
    tile = weights[0].shape[0] // tiles
    width = tile * len(weights)

    def kernel(place_ref, mine_ref, other_ref, *refs):
        weight_refs = refs[: len(weights)]
        kept_ref, sent_ref, context = refs[len(weights) :]
        core, plane = place_ref[1], place_ref[2]

        @pl.when(pl.program_id(0) == 0)
        def _():
            for n, step in enumerate((0, 2, 1, 3)):
                begin = pl.multiple_of((plane ^ step) * quarter, quarter)
                here = slice(n * quarter, (n + 1) * quarter)
                for ref, which in ((mine_ref, core), (other_ref, 1 - core)):
                    lanes = pl.ds(pl.multiple_of(which * half, half), half)
                    context[here, lanes] = ref[pl.ds(begin, quarter), :]

        for n, ref in enumerate(weight_refs):
            part = lax.dot_general(
                context[...],
                ref[...],
                (((1,), (1,)), ((), ())),
                preferred_element_type=jnp.float32,
            )
            here = slice(n * tile, (n + 1) * tile)
            kept_ref[:, here] = part[: 2 * quarter]
            sent_ref[:, here] = part[2 * quarter :].astype(jnp.bfloat16)

    def whole(a):
        return pl.BlockSpec(a.shape, lambda t: (0, 0))

    return pl.pallas_call(
        kernel,
        grid=(tiles,),
        out_shape=[
            jax.ShapeDtypeStruct((2 * quarter, tiles * width), kind)
            for kind in (jnp.float32, jnp.bfloat16)
        ],
        in_specs=[smem_spec(), whole(mine), whole(other)]
        + [pl.BlockSpec((tile, 2 * half), lambda t: (t, 0))] * len(weights),
        out_specs=[pl.BlockSpec((2 * quarter, width), lambda t: (0, t))] * 2,
        scratch_shapes=[pltpu.VMEM((rows, 2 * half), jnp.bfloat16)],
        compiler_params=pltpu.CompilerParams(vmem_limit_bytes=VMEM),
        cost_estimate=pl.CostEstimate(
            flops=2 * rows * 2 * half * width * tiles,
            bytes_accessed=2 * width * tiles * 2 * half,
            transcendentals=0,
        ),
        name="project_out",
    )(place, mine, other, *weights)


def add_up(place, groups, shard, tiles=2):
    rows, width = groups[0][3].shape
    tile = shard // tiles

    def kernel(place_ref, *refs):
        out_ref = refs[-1]
        for n, (owners, *_) in enumerate(groups):
            kept_ref, first_ref, second_ref = refs[3 * n : 3 * n + 3]
            total = kept_ref[...] + first_ref[...].astype(jnp.float32)
            total = total + second_ref[...].astype(jnp.float32)
            for i, whose in enumerate(owners):
                chip_at, core_at = owner(place_ref, whose)
                for t in range(tiles):
                    begin = (chip_at * 2 + core_at) * shard + t * tile
                    at = (t * len(owners) + i) * tile
                    out_ref[:, pl.ds(pl.multiple_of(begin, tile), tile)] = total[
                        :, at : at + tile
                    ].astype(jnp.bfloat16)

    args = [a for group in groups for a in group[1:]]
    return pl.pallas_call(
        kernel,
        out_shape=jax.ShapeDtypeStruct((rows, 8 * shard), jnp.bfloat16),
        grid=(1,),
        in_specs=[smem_spec()] + [pl.BlockSpec((rows, width), lambda t: (0, 0))] * len(args),
        out_specs=pl.BlockSpec((rows, 8 * shard), lambda t: (0, 0)),
        compiler_params=pltpu.CompilerParams(vmem_limit_bytes=VMEM),
        cost_estimate=pl.CostEstimate(
            flops=2 * rows * 8 * shard, bytes_accessed=8 * rows * 8 * shard, transcendentals=0
        ),
        name="add_up",
    )(place, *args)


def plane_shards(decoder_states, w_query, w_out_t, enc_keys, enc_values):
    block, plane = lax.axis_index("blk"), lax.axis_index("fsdp")
    chip, core = block // 2, block % 2
    place = jnp.stack([chip, core, plane]).astype(jnp.int32)
    shard = w_query.shape[0]
    half = enc_keys.shape[1] // 2

    states_2 = over_z(decoder_states, 2)
    states_1 = over_z(decoder_states, 1)
    states_3 = over_z(states_2, 1)

    near, side = cross(w_query), cross_back(w_query)
    far = cross(after(side, near, states_1, states_2))
    query_pieces = [
        (OWN, w_query),
        (OWN_SWAPPED, over_core(w_query)),
        (NEAR, near),
        (NEAR_SWAPPED, over_core(near)),
        (SIDE, side),
        (SIDE_SWAPPED, over_core(side)),
        (FAR, far),
        (FAR_SWAPPED, over_core(far)),
    ]

    def columns(a, which):
        return lax.dynamic_slice_in_dim(a, which * half, half, 1)

    def side_by_side(which):
        return jnp.concatenate([columns(enc_keys, which), columns(enc_values, which)], axis=1)

    swapped = over_core(side_by_side(1 - core))
    encoded = jnp.concatenate([side_by_side(core), swapped], axis=0)
    encoded_near = cross(after(encoded, near, side, states_1, states_2))

    queries, queries_other = project_queries(
        place,
        [decoder_states, states_1, states_2, states_3],
        query_pieces,
    )
    encoded_passed = cross(after(over_core(encoded), far, states_3))
    encoded_far = cross_back(after(encoded_near, queries))
    query_blocks = [queries, over_core(queries_other)]
    before = attend(query_blocks, [encoded, encoded_near])
    encoded_side = over_core(after(encoded_passed, before[0][0]))
    context, context_other = attend(query_blocks, [encoded_side, encoded_far], before)
    context_back = over_core(context_other)

    out_own = after(w_out_t, encoded_passed, before[0][0])
    out_near = cross_back(out_own)
    out_side = cross(after(w_out_t, encoded_far))
    sums = []

    def add_group(*group):
        pieces = [piece for _, piece in group]
        kept, sent = project_out(place, context, context_back, pieces)
        first = over_z(sent, 1)
        rows = kept.shape[0] // 2
        passed = (kept[rows:] + first[rows:].astype(jnp.float32)).astype(jnp.bfloat16)
        second = over_z(passed, 2)
        sums.append(([whose for whose, _ in group], kept, first, second))
        return sent, passed, second

    sent, passed, second = add_group((OWN, w_out_t), (OWN_SWAPPED, over_core(out_own)))
    sent, passed_next, _ = add_group((SIDE, out_near), (SIDE_SWAPPED, over_core(after(out_near, context))))
    out_far = cross(after(out_near, sent))
    out_side = after(out_side, passed)
    add_group((NEAR, out_side), (NEAR_SWAPPED, over_core(out_side)))
    out_far = after(out_far, passed_next, second)
    add_group((FAR, out_far), (FAR_SWAPPED, over_core(out_far)))
    return add_up(place, sums, shard)


def solution(mesh):
    in_specs = (
        P("blk", "fsdp"),
        P("blk", "fsdp"),
        P("blk", "fsdp"),
        P("blk", "fsdp"),
        P("blk", "fsdp"),
    )
    out_specs = P(("blk", "fsdp"), None)
    by_planes = mesh.shape["blk"] == 8 and mesh.shape["fsdp"] == 4
    return jax.shard_map(
        plane_shards if by_planes else gathered_shards,
        mesh=mesh,
        in_specs=in_specs,
        out_specs=out_specs,
        check_vma=False,
    )
```

```python
import math

import jax
import jax.numpy as jnp
from jax import lax
from jax.experimental import pallas as pl
from jax.experimental.pallas import tpu as pltpu
from jax.sharding import PartitionSpec as P

HEAD_DIM = 64
PAIR = 2 * HEAD_DIM
PAIRS_AT_ONCE = 2
VMEM = 60 * 1024 * 1024


def absorb(fold_state, query_heads, key_rows, value_rows):
    running_top, running_sum, weighted = fold_state
    local_heads = query_heads.shape[1]
    key_heads = key_rows.reshape(key_rows.shape[0], local_heads, HEAD_DIM)
    value_heads = value_rows.reshape(value_rows.shape[0], local_heads, HEAD_DIM)
    scores = jnp.einsum(
        "qhd,khd->hqk", query_heads, key_heads, preferred_element_type=jnp.float32
    ) * (1.0 / math.sqrt(HEAD_DIM))
    new_top = jnp.max(scores, axis=2)
    rescale = jnp.exp(running_top - new_top)
    probability = jnp.exp(scores - new_top[:, :, None])
    running_sum = running_sum * rescale + jnp.sum(probability, axis=2)
    weighted = weighted * rescale[:, :, None] + jnp.einsum(
        "hqk,khd->hqd",
        probability.astype(jnp.bfloat16),
        value_heads,
        preferred_element_type=jnp.float32,
    )
    return (new_top, running_sum, weighted)


def gathered_shards(decoder_states, w_query, w_out_t, enc_keys, enc_values):
    query_full = lax.all_gather(w_query, "blk", axis=0, tiled=True)
    row_count = decoder_states.shape[0]
    columns = query_full.shape[1]
    local_heads = columns // HEAD_DIM
    queries = jnp.dot(
        lax.all_gather(decoder_states, "fsdp", axis=1, tiled=True),
        query_full,
        preferred_element_type=jnp.float32,
    ).astype(jnp.bfloat16)
    start_state = (
        jnp.full((local_heads, row_count), -jnp.inf, jnp.float32),
        jnp.zeros((local_heads, row_count), jnp.float32),
        jnp.zeros((local_heads, row_count, HEAD_DIM), jnp.float32),
    )
    query_heads = queries.reshape(row_count, local_heads, HEAD_DIM)
    final_state = absorb(
        start_state,
        query_heads,
        lax.all_gather(enc_keys, "blk", axis=0, tiled=True),
        lax.all_gather(enc_values, "blk", axis=0, tiled=True),
    )
    context = final_state[2] / final_state[1][:, :, None]
    context = jnp.transpose(context, (1, 0, 2)).reshape(row_count, columns).astype(jnp.bfloat16)
    out_full = lax.all_gather(w_out_t, "blk", axis=0, tiled=True)
    return lax.psum_scatter(
        lax.dot_general(
            context, out_full, (((1,), (1,)), ((), ())), preferred_element_type=jnp.float32
        ),
        "fsdp",
        scatter_dimension=0,
        tiled=True,
    ).astype(jnp.bfloat16)


CORE = [(b, b ^ 1) for b in range(8)]
CROSS = [(b, b ^ (2 if b % 2 == 0 else 4)) for b in range(8)]
CROSS_BACK = [(b, b ^ (4 if b % 2 == 0 else 2)) for b in range(8)]

def over_core(a):
    return lax.ppermute(a, "blk", CORE)


def cross(a):
    return lax.ppermute(a, "blk", CROSS)


def cross_back(a):
    return lax.ppermute(a, "blk", CROSS_BACK)


def over_z(a, step):
    return lax.ppermute(a, "fsdp", [(z, z ^ step) for z in range(4)])


def over_core_and_z(a, step):
    pairs = [(b * 4 + z, (b ^ 1) * 4 + (z ^ step)) for b in range(8) for z in range(4)]
    return lax.ppermute(a, ("blk", "fsdp"), pairs)


def after(value, *earlier):
    return lax.optimization_barrier((value,) + earlier)[0]


OWN, NEAR, SIDE, FAR = (0, 0), (1, 2), (2, 1), (3, 3)


def chip_of(place_ref, whose, core_step=0):
    chip, core = place_ref[0], place_ref[1] ^ core_step
    even, odd = whose
    return chip ^ (even + core * (odd - even))


def any_spec():
    return pl.BlockSpec(memory_space=pl.ANY)


def smem_spec():
    return pl.BlockSpec(memory_space=pltpu.SMEM)


def vmem_spec():
    return pl.BlockSpec(memory_space=pltpu.VMEM)


def project_queries(place, states, weights):
    rows, depth = states[0].shape
    columns = weights[0][1].shape[1]
    shard = depth // 2

    def kernel(place_ref, *refs):
        state_refs = refs[: len(states)]
        weight_refs = refs[len(states) : len(states) + len(weights)]
        mine_ref, other_ref, state_s, weight_s, total, sems = refs[len(states) + len(weights) :]
        core, plane = place_ref[1], place_ref[2]
        chips = [chip_of(place_ref, whose) for whose, _ in weights]

        def copy_states(which, n):
            here = pl.ds(n // 4 * rows, rows)
            sem = sems.at[n // 4, plane ^ (n % 4)] if which is None else sems.at[n // 4, which]
            at = plane ^ (n % 4) if which is None else which
            return pltpu.make_async_copy(state_refs[n], state_s.at[at, here], sem)

        def copy_weights(n, part):
            begin = pl.multiple_of((core ^ part) * shard, shard)
            return pltpu.make_async_copy(
                weight_refs[n].at[pl.ds(part * shard, shard)],
                weight_s.at[chips[n], pl.ds(begin, shard)],
                sems.at[2 + part, n],
            )

        for n in range(4):
            copy_states(None, n).start()
            copy_states(None, n + 4).start()
            copy_weights(n, 0).start()
            copy_weights(n, 1).start()
        for n, chip_at in enumerate(chips):
            copy_states(chip_at, 0).wait()
            copy_states(chip_at, 4).wait()
            copy_weights(n, 0).wait()
            copy_weights(n, 1).wait()
            part = jnp.dot(state_s[chip_at], weight_s[chip_at], preferred_element_type=jnp.float32)
            total[...] = part if n == 0 else total[...] + part
        factor = 1.0 / math.sqrt(HEAD_DIM)
        for ref, first in ((mine_ref, 0), (other_ref, rows)):
            queries = total[first : first + rows].astype(jnp.bfloat16)
            ref[...] = (queries.astype(jnp.float32) * factor).astype(jnp.bfloat16)

    shape = jax.ShapeDtypeStruct((rows, columns), jnp.bfloat16)
    return pl.pallas_call(
        kernel,
        out_shape=(shape, shape),
        in_specs=[smem_spec()] + [any_spec()] * (len(states) + len(weights)),
        out_specs=(vmem_spec(), vmem_spec()),
        scratch_shapes=[
            pltpu.VMEM((4, 2 * rows, depth), jnp.bfloat16),
            pltpu.VMEM((4, depth, columns), jnp.bfloat16),
            pltpu.VMEM((2 * rows, columns), jnp.float32),
            pltpu.SemaphoreType.DMA((4, 4)),
        ],
        compiler_params=pltpu.CompilerParams(vmem_limit_bytes=VMEM),
        cost_estimate=pl.CostEstimate(
            flops=4 * rows * 4 * depth * columns,
            bytes_accessed=2 * 4 * depth * (2 * rows + columns),
            transcendentals=0,
        ),
        name="project_queries",
    )(place, *states, *[w[1] for w in weights])


def pair_part(queries, keys, values):
    rows = queries.shape[0]
    first = lax.broadcasted_iota(jnp.int32, (rows, PAIR), 1) < HEAD_DIM
    found = []
    for head in range(2):
        masked = jnp.where(first if head == 0 else jnp.logical_not(first), queries, 0)
        scores = [
            lax.dot_general(
                masked, k, (((1,), (1,)), ((), ())), preferred_element_type=jnp.float32
            )
            for k in keys
        ]
        top = scores[0].max(axis=1, keepdims=True)
        for s in scores[1:]:
            top = jnp.maximum(top, s.max(axis=1, keepdims=True))
        both = None
        for s, v in zip(scores, values):
            probability = jnp.exp(s - top).astype(jnp.bfloat16)
            part = jnp.dot(probability, v, preferred_element_type=jnp.float32)
            both = part if both is None else both + part
        found.append((both[:, :PAIR], both[:, PAIR:], jnp.broadcast_to(top, (rows, PAIR))))
    return [jnp.where(first, a, b) for a, b in zip(*found)]


def attend(query_blocks, pieces, before=None):
    rows, columns = query_blocks[0].shape
    width = PAIRS_AT_ONCE * PAIR
    steps = columns // width
    blocks = len(query_blocks)
    last = before is not None
    held = [] if before is None else [a for block in before for a in block]
    outs = 1 if last else 3 * blocks

    def kernel(*refs):
        refs = list(refs)
        q_refs = [refs.pop(0) for _ in range(blocks)]
        k_refs = [refs.pop(0) for _ in pieces]
        v_refs = [refs.pop(0) for _ in pieces]
        held_refs = [refs.pop(0) for _ in held]
        out_refs = [refs.pop(0) for _ in range(outs)]
        for pair in range(PAIRS_AT_ONCE):
            at = slice(pair * PAIR, (pair + 1) * PAIR)
            ks = [r[:, at] for r in k_refs]
            ones = [jnp.ones((r.shape[0], PAIR), jnp.bfloat16) for r in v_refs]
            vs = [jnp.concatenate([r[:, at], one], axis=1) for r, one in zip(v_refs, ones)]
            for n in range(blocks):
                weighted, sums, tops = pair_part(q_refs[n][:, at], ks, vs)
                if last:
                    weighted_0, sums_0, tops_0 = (r[:, at] for r in held_refs[3 * n : 3 * n + 3])
                    top = jnp.maximum(tops, tops_0)
                    now, then = jnp.exp(tops - top), jnp.exp(tops_0 - top)
                    weighted = weighted * now + weighted_0 * then
                    sums = sums * now + sums_0 * then
                    out_refs[0][n, :, at] = (weighted / sums).astype(jnp.bfloat16)
                else:
                    for ref, a in zip(out_refs[3 * n : 3 * n + 3], (weighted, sums, tops)):
                        ref[:, at] = a

    def spec(a, skip=0):
        return pl.BlockSpec((a.shape[0], width), lambda p: (0, p + skip))

    args = list(query_blocks) + list(pieces) + list(pieces) + held
    in_specs = (
        [spec(a) for a in query_blocks]
        + [spec(a) for a in pieces]
        + [spec(a, steps) for a in pieces]
        + [spec(a) for a in held]
    )
    out_shape = [jax.ShapeDtypeStruct((rows, columns), jnp.float32)] * outs
    out_specs = [spec(a) for a in out_shape]
    if last:
        out_shape = [jax.ShapeDtypeStruct((blocks, rows, columns), jnp.bfloat16)]
        out_specs = [pl.BlockSpec((blocks, rows, width), lambda p: (0, 0, p))]
    total_keys = sum(a.shape[0] for a in pieces)
    found = pl.pallas_call(
        kernel,
        grid=(steps,),
        out_shape=out_shape,
        in_specs=in_specs,
        out_specs=out_specs,
        compiler_params=pltpu.CompilerParams(vmem_limit_bytes=VMEM),
        cost_estimate=pl.CostEstimate(
            flops=2 * 2 * blocks * rows * total_keys * columns * 4,
            bytes_accessed=sum(a.size * a.dtype.itemsize for a in args),
            transcendentals=blocks * rows * total_keys * (columns // HEAD_DIM),
        ),
        name="attend_last" if last else "attend_first",
    )(*args)
    if last:
        return found[0]
    return [found[3 * n : 3 * n + 3] for n in range(blocks)]


def project_out(place, mine, got, weights, tiles=2):
    blocks, rows, half = mine.shape
    quarter = rows // 4
    tile = weights.shape[0] // tiles
    held = blocks * rows // 2

    def kernel(place_ref, mine_ref, got_ref, weight_ref, kept_ref, sent_ref, context):
        core, plane = place_ref[1], place_ref[2]

        @pl.when(pl.program_id(0) == 0)
        def _():
            for n, step in enumerate((0, 2, 1, 3)):
                begin = pl.ds(pl.multiple_of((plane ^ step) * quarter, quarter), quarter)
                for i in range(blocks):
                    here = pl.ds((n * blocks + i) * quarter, quarter)
                    lanes = pl.ds(pl.multiple_of(core * half, half), half)
                    context[here, lanes] = mine_ref[i, begin]
                    lanes = pl.ds(pl.multiple_of((1 - core) * half, half), half)
                    context[here, lanes] = got_ref[1 - i, begin]

        part = lax.dot_general(
            context[...],
            weight_ref[...],
            (((1,), (1,)), ((), ())),
            preferred_element_type=jnp.float32,
        )
        kept_ref[...] = part[:held]
        sent_ref[...] = part[held:].astype(jnp.bfloat16)

    def whole(a):
        return pl.BlockSpec(a.shape, lambda t: (0, 0, 0))

    return pl.pallas_call(
        kernel,
        grid=(tiles,),
        out_shape=[
            jax.ShapeDtypeStruct((held, tiles * tile), kind) for kind in (jnp.float32, jnp.bfloat16)
        ],
        in_specs=[
            smem_spec(),
            whole(mine),
            whole(got),
            pl.BlockSpec((tile, 2 * half), lambda t: (t, 0)),
        ],
        out_specs=[pl.BlockSpec((held, tile), lambda t: (0, t))] * 2,
        scratch_shapes=[pltpu.VMEM((2 * held, 2 * half), jnp.bfloat16)],
        compiler_params=pltpu.CompilerParams(vmem_limit_bytes=VMEM),
        cost_estimate=pl.CostEstimate(
            flops=2 * 2 * held * 2 * half * tile * tiles,
            bytes_accessed=2 * tile * tiles * 2 * half,
            transcendentals=0,
        ),
        name="project_out",
    )(place, mine, got, weights)


def add_up(groups):
    rows, width = groups[0][2].shape
    rows //= 2

    def kernel(*refs):
        own_ref, other_ref = refs[-2:]
        for n in range(len(groups)):
            kept_ref, first_ref, second_ref = refs[3 * n : 3 * n + 3]
            total = kept_ref[...] + first_ref[...].astype(jnp.float32)
            total = (total + second_ref[...].astype(jnp.float32)).astype(jnp.bfloat16)
            here = slice(n * width, (n + 1) * width)
            own_ref[:, here] = total[:rows]
            other_ref[:, here] = total[rows:]

    args = [a for group in groups for a in group]
    shape = jax.ShapeDtypeStruct((rows, len(groups) * width), jnp.bfloat16)
    return pl.pallas_call(
        kernel,
        grid=(1,),
        out_shape=(shape, shape),
        in_specs=[pl.BlockSpec((2 * rows, width), lambda t: (0, 0))] * len(args),
        out_specs=[pl.BlockSpec(shape.shape, lambda t: (0, 0))] * 2,
        compiler_params=pltpu.CompilerParams(vmem_limit_bytes=VMEM),
        cost_estimate=pl.CostEstimate(
            flops=4 * rows * shape.shape[1],
            bytes_accessed=20 * rows * shape.shape[1],
            transcendentals=0,
        ),
        name="add_up",
    )(*args)


def put_in_place(place, chips, mine, got, last):
    rows = mine.shape[0]
    shard = mine.shape[1] // (len(chips) - 1)

    def kernel(place_ref, *refs):
        out_ref = refs[-1]
        for n, whose in enumerate(chips):
            for core_step in range(2):
                if n < len(chips) - 1:
                    value = refs[core_step][:, n * shard : (n + 1) * shard]
                else:
                    near_ref, away_ref = refs[2 + 2 * core_step : 4 + 2 * core_step]
                    value = near_ref[...] + away_ref[...].astype(jnp.float32)
                at = chip_of(place_ref, whose, core_step) * 2 + (place_ref[1] ^ core_step)
                begin = pl.multiple_of(at * shard, shard)
                out_ref[:, pl.ds(begin, shard)] = value.astype(jnp.bfloat16)

    args = [mine, got, *last]
    return pl.pallas_call(
        kernel,
        out_shape=jax.ShapeDtypeStruct((rows, 8 * shard), jnp.bfloat16),
        in_specs=[smem_spec()] + [vmem_spec()] * len(args),
        out_specs=vmem_spec(),
        compiler_params=pltpu.CompilerParams(vmem_limit_bytes=VMEM),
        cost_estimate=pl.CostEstimate(
            flops=0, bytes_accessed=4 * rows * 8 * shard, transcendentals=0
        ),
        name="put_in_place",
    )(place, *args)


def plane_shards(decoder_states, w_query, w_out_t, enc_keys, enc_values):
    block, plane = lax.axis_index("blk"), lax.axis_index("fsdp")
    core = block % 2
    place = jnp.stack([block // 2, core, plane]).astype(jnp.int32)
    shard, rows = w_query.shape[0], enc_keys.shape[0]

    def half_of(a, which):
        width = a.shape[1] // 2
        return lax.dynamic_slice_in_dim(a, which * width, width, 1)

    def whole_rows(a, got):
        return jnp.concatenate([half_of(a, core), got])

    def add_passed(sums, first):
        begin = sums[0].shape[0] // 2
        return (sums[0][begin:] + first[begin:].astype(jnp.float32)).astype(jnp.bfloat16)

    def totals(sums, first):
        own, other, same, crossed = jnp.split(sums[0] + first.astype(jnp.float32), 4)
        return own, other, same.astype(jnp.bfloat16), crossed.astype(jnp.bfloat16)

    states_1 = over_z(decoder_states, 1)
    states_2 = over_z(decoder_states, 2)
    states_3 = over_z(states_2, 1)
    others = over_core(decoder_states)
    others_1 = over_core(after(states_1, others))
    others_2 = over_core(after(states_2, others_1))
    others_3 = over_core(after(states_3, others_2))
    to_swap = jnp.concatenate([half_of(a, 1 - core) for a in (w_query, enc_keys, enc_values)])
    swapped = over_core(to_swap)
    weights = jnp.concatenate([half_of(w_query, core), swapped[:shard]])
    near_weights = cross(weights)
    side_weights = cross_back(weights)
    far_weights = cross_back(after(near_weights, near_weights, side_weights, states_1, states_2))
    queries = project_queries(place, [decoder_states, states_1, states_2, states_3, others, others_1, others_2, others_3], [(OWN, weights), (NEAR, near_weights), (SIDE, side_weights), (FAR, far_weights)])
    encoded = jnp.concatenate([whole_rows(enc_keys, swapped[shard:-rows]), whole_rows(enc_values, swapped[-rows:])], axis=1)
    near_encoded = cross(after(encoded, states_1))
    before = attend(queries, [encoded, near_encoded])
    side_encoded = cross_back(after(encoded, states_1, states_2, others_1))
    far_encoded = cross_back(near_encoded)
    context = attend(queries, [side_encoded, far_encoded], before)
    context_got = over_core(context)
    sums_0 = project_out(place, context, context_got, w_out_t)
    first_0 = over_z(sums_0[1], 1)
    near_out = cross(after(w_out_t, context))
    passed_0 = add_passed(after(sums_0, context_got, near_out), first_0)
    side_out = cross_back(after(w_out_t, before))
    sums_1 = project_out(place, after(context, sums_0), context_got, side_out)
    first_1 = over_z(sums_1[1], 1)
    second_0 = over_z(after(passed_0, first_1), 2)
    passed_1 = add_passed(sums_1, first_1)
    second_1 = over_z(passed_1, 2)
    sums_2 = project_out(place, after(context, sums_1), context_got, near_out)
    first_2 = over_z(sums_2[1], 1)
    far_out = cross(side_out)
    passed_2 = add_passed(after(sums_2, far_out), first_2)
    second_2 = over_z(passed_2, 2)
    most_added = add_up([(sums_0[0], first_0, second_0), (sums_1[0], first_1, second_1), (sums_2[0], first_2, second_2)])
    most_got = over_core(most_added[1])
    sums_3 = project_out(place, after(context, sums_2), context_got, far_out)
    first_3 = over_z(sums_3[1], 1)
    passed_3 = totals(sums_3, first_3)
    second_3 = over_z(passed_3[2], 2)
    last_got = over_core(passed_3[1])
    third_3 = over_core_and_z(after(passed_3, first_2)[3], 2)
    return put_in_place(place, (OWN, SIDE, NEAR, FAR), most_added[0], most_got, (passed_3[0], second_3, last_got, third_3))


def solution(mesh):
    in_specs = (
        P("blk", "fsdp"),
        P("blk", "fsdp"),
        P("blk", "fsdp"),
        P("blk", "fsdp"),
        P("blk", "fsdp"),
    )
    out_specs = P(("blk", "fsdp"), None)
    by_planes = mesh.shape["blk"] == 8 and mesh.shape["fsdp"] == 4
    return jax.shard_map(
        plane_shards if by_planes else gathered_shards,
        mesh=mesh,
        in_specs=in_specs,
        out_specs=out_specs,
        check_vma=False,
    )
```

```python
import math

import jax
import jax.numpy as jnp
from jax import lax
from jax.experimental import pallas as pl
from jax.experimental.pallas import tpu as pltpu
from jax.sharding import PartitionSpec as P

HEAD_DIM = 64
PAIR = 2 * HEAD_DIM
PAIRS_AT_ONCE = 2
VMEM = 60 * 1024 * 1024


def absorb(fold_state, query_heads, key_rows, value_rows):
    running_top, running_sum, weighted = fold_state
    local_heads = query_heads.shape[1]
    key_heads = key_rows.reshape(key_rows.shape[0], local_heads, HEAD_DIM)
    value_heads = value_rows.reshape(value_rows.shape[0], local_heads, HEAD_DIM)
    scores = jnp.einsum(
        "qhd,khd->hqk", query_heads, key_heads, preferred_element_type=jnp.float32
    ) * (1.0 / math.sqrt(HEAD_DIM))
    new_top = jnp.max(scores, axis=2)
    rescale = jnp.exp(running_top - new_top)
    probability = jnp.exp(scores - new_top[:, :, None])
    running_sum = running_sum * rescale + jnp.sum(probability, axis=2)
    weighted = weighted * rescale[:, :, None] + jnp.einsum(
        "hqk,khd->hqd",
        probability.astype(jnp.bfloat16),
        value_heads,
        preferred_element_type=jnp.float32,
    )
    return (new_top, running_sum, weighted)


def gathered_shards(decoder_states, w_query, w_out_t, enc_keys, enc_values):
    query_full = lax.all_gather(w_query, "blk", axis=0, tiled=True)
    row_count = decoder_states.shape[0]
    columns = query_full.shape[1]
    local_heads = columns // HEAD_DIM
    queries = jnp.dot(
        lax.all_gather(decoder_states, "fsdp", axis=1, tiled=True),
        query_full,
        preferred_element_type=jnp.float32,
    ).astype(jnp.bfloat16)
    start_state = (
        jnp.full((local_heads, row_count), -jnp.inf, jnp.float32),
        jnp.zeros((local_heads, row_count), jnp.float32),
        jnp.zeros((local_heads, row_count, HEAD_DIM), jnp.float32),
    )
    query_heads = queries.reshape(row_count, local_heads, HEAD_DIM)
    final_state = absorb(
        start_state,
        query_heads,
        lax.all_gather(enc_keys, "blk", axis=0, tiled=True),
        lax.all_gather(enc_values, "blk", axis=0, tiled=True),
    )
    context = final_state[2] / final_state[1][:, :, None]
    context = jnp.transpose(context, (1, 0, 2)).reshape(row_count, columns).astype(jnp.bfloat16)
    out_full = lax.all_gather(w_out_t, "blk", axis=0, tiled=True)
    return lax.psum_scatter(
        lax.dot_general(
            context, out_full, (((1,), (1,)), ((), ())), preferred_element_type=jnp.float32
        ),
        "fsdp",
        scatter_dimension=0,
        tiled=True,
    ).astype(jnp.bfloat16)


CORE = [(b, b ^ 1) for b in range(8)]
CROSS = [(b, b ^ (2 if b % 2 == 0 else 4)) for b in range(8)]
CROSS_BACK = [(b, b ^ (4 if b % 2 == 0 else 2)) for b in range(8)]

def over_core(a):
    return lax.ppermute(a, "blk", CORE)


def cross(a):
    return lax.ppermute(a, "blk", CROSS)


def cross_back(a):
    return lax.ppermute(a, "blk", CROSS_BACK)


def over_z(a, step):
    return lax.ppermute(a, "fsdp", [(z, z ^ step) for z in range(4)])


def after(value, *earlier):
    return lax.optimization_barrier((value,) + earlier)[0]


OWN, NEAR, SIDE, FAR = (0, 0), (1, 2), (2, 1), (3, 3)


def chip_of(place_ref, whose, core_step=0):
    chip, core = place_ref[0], place_ref[1] ^ core_step
    even, odd = whose
    return chip ^ (even + core * (odd - even))


def any_spec():
    return pl.BlockSpec(memory_space=pl.ANY)


def smem_spec():
    return pl.BlockSpec(memory_space=pltpu.SMEM)


def vmem_spec():
    return pl.BlockSpec(memory_space=pltpu.VMEM)


def project_queries(place, states, weights):
    rows, depth = states[0].shape
    columns = weights[0][1].shape[1]
    shard = depth // 2

    def kernel(place_ref, *refs):
        state_refs = refs[: len(states)]
        weight_refs = refs[len(states) : len(states) + len(weights)]
        mine_ref, other_ref, state_s, weight_s, total, sems = refs[len(states) + len(weights) :]
        core, plane = place_ref[1], place_ref[2]
        chips = [chip_of(place_ref, whose) for whose, _ in weights]

        def copy_states(which, n):
            here = pl.ds(n // 4 * rows, rows)
            sem = sems.at[n // 4, plane ^ (n % 4)] if which is None else sems.at[n // 4, which]
            at = plane ^ (n % 4) if which is None else which
            return pltpu.make_async_copy(state_refs[n], state_s.at[at, here], sem)

        def copy_weights(n, part):
            begin = pl.multiple_of((core ^ part) * shard, shard)
            return pltpu.make_async_copy(
                weight_refs[n].at[pl.ds(part * shard, shard)],
                weight_s.at[chips[n], pl.ds(begin, shard)],
                sems.at[2 + part, n],
            )

        for n in range(4):
            copy_states(None, n).start()
            copy_states(None, n + 4).start()
            copy_weights(n, 0).start()
            copy_weights(n, 1).start()
        for n, chip_at in enumerate(chips):
            copy_states(chip_at, 0).wait()
            copy_states(chip_at, 4).wait()
            copy_weights(n, 0).wait()
            copy_weights(n, 1).wait()
            part = jnp.dot(state_s[chip_at], weight_s[chip_at], preferred_element_type=jnp.float32)
            total[...] = part if n == 0 else total[...] + part
        factor = 1.0 / math.sqrt(HEAD_DIM)
        for ref, first in ((mine_ref, 0), (other_ref, rows)):
            queries = total[first : first + rows].astype(jnp.bfloat16)
            ref[...] = (queries.astype(jnp.float32) * factor).astype(jnp.bfloat16)

    shape = jax.ShapeDtypeStruct((rows, columns), jnp.bfloat16)
    return pl.pallas_call(
        kernel,
        out_shape=(shape, shape),
        in_specs=[smem_spec()] + [any_spec()] * (len(states) + len(weights)),
        out_specs=(vmem_spec(), vmem_spec()),
        scratch_shapes=[
            pltpu.VMEM((4, 2 * rows, depth), jnp.bfloat16),
            pltpu.VMEM((4, depth, columns), jnp.bfloat16),
            pltpu.VMEM((2 * rows, columns), jnp.float32),
            pltpu.SemaphoreType.DMA((4, 4)),
        ],
        compiler_params=pltpu.CompilerParams(vmem_limit_bytes=VMEM),
        cost_estimate=pl.CostEstimate(
            flops=4 * rows * 4 * depth * columns,
            bytes_accessed=2 * 4 * depth * (2 * rows + columns),
            transcendentals=0,
        ),
        name="project_queries",
    )(place, *states, *[w[1] for w in weights])


def pair_part(queries, keys, values):
    rows = queries.shape[0]
    first = lax.broadcasted_iota(jnp.int32, (rows, PAIR), 1) < HEAD_DIM
    found = []
    for head in range(2):
        masked = jnp.where(first if head == 0 else jnp.logical_not(first), queries, 0)
        scores = [
            lax.dot_general(
                masked, k, (((1,), (1,)), ((), ())), preferred_element_type=jnp.float32
            )
            for k in keys
        ]
        top = scores[0].max(axis=1, keepdims=True)
        for s in scores[1:]:
            top = jnp.maximum(top, s.max(axis=1, keepdims=True))
        both = None
        for s, v in zip(scores, values):
            probability = jnp.exp(s - top).astype(jnp.bfloat16)
            part = jnp.dot(probability, v, preferred_element_type=jnp.float32)
            both = part if both is None else both + part
        found.append((both[:, :PAIR], both[:, PAIR:], jnp.broadcast_to(top, (rows, PAIR))))
    return [jnp.where(first, a, b) for a, b in zip(*found)]


def attend(query_blocks, pieces, before=None, last=True):
    rows, columns = query_blocks[0].shape
    width = PAIRS_AT_ONCE * PAIR
    steps = columns // width
    blocks = len(query_blocks)
    last = last and before is not None
    held = [] if before is None else [a for block in before for a in block]
    outs = 1 if last else 3 * blocks

    def kernel(*refs):
        refs = list(refs)
        q_refs = [refs.pop(0) for _ in range(blocks)]
        k_refs = [refs.pop(0) for _ in pieces]
        v_refs = [refs.pop(0) for _ in pieces]
        held_refs = [refs.pop(0) for _ in held]
        out_refs = [refs.pop(0) for _ in range(outs)]
        for pair in range(PAIRS_AT_ONCE):
            at = slice(pair * PAIR, (pair + 1) * PAIR)
            ks = [r[:, at] for r in k_refs]
            ones = [jnp.ones((r.shape[0], PAIR), jnp.bfloat16) for r in v_refs]
            vs = [jnp.concatenate([r[:, at], one], axis=1) for r, one in zip(v_refs, ones)]
            for n in range(blocks):
                weighted, sums, tops = pair_part(q_refs[n][:, at], ks, vs)
                if held:
                    weighted_0, sums_0, tops_0 = (r[:, at] for r in held_refs[3 * n : 3 * n + 3])
                    top = jnp.maximum(tops, tops_0)
                    now, then = jnp.exp(tops - top), jnp.exp(tops_0 - top)
                    weighted = weighted * now + weighted_0 * then
                    sums = sums * now + sums_0 * then
                    tops = top
                if last:
                    out_refs[0][n, :, at] = (weighted / sums).astype(jnp.bfloat16)
                else:
                    for ref, a in zip(out_refs[3 * n : 3 * n + 3], (weighted, sums, tops)):
                        ref[:, at] = a

    def spec(a, skip=0):
        return pl.BlockSpec((a.shape[0], width), lambda p: (0, p + skip))

    args = list(query_blocks) + list(pieces) + list(pieces) + held
    in_specs = (
        [spec(a) for a in query_blocks]
        + [spec(a) for a in pieces]
        + [spec(a, steps) for a in pieces]
        + [spec(a) for a in held]
    )
    out_shape = [jax.ShapeDtypeStruct((rows, columns), jnp.float32)] * outs
    out_specs = [spec(a) for a in out_shape]
    if last:
        out_shape = [jax.ShapeDtypeStruct((blocks, rows, columns), jnp.bfloat16)]
        out_specs = [pl.BlockSpec((blocks, rows, width), lambda p: (0, 0, p))]
    total_keys = sum(a.shape[0] for a in pieces)
    found = pl.pallas_call(
        kernel,
        grid=(steps,),
        out_shape=out_shape,
        in_specs=in_specs,
        out_specs=out_specs,
        compiler_params=pltpu.CompilerParams(vmem_limit_bytes=VMEM),
        cost_estimate=pl.CostEstimate(
            flops=2 * 2 * blocks * rows * total_keys * columns * 4,
            bytes_accessed=sum(a.size * a.dtype.itemsize for a in args),
            transcendentals=blocks * rows * total_keys * (columns // HEAD_DIM),
        ),
        name=f"attend_{'last' if last else 'next' if held else 'first'}_{len(pieces)}",
    )(*args)
    if last:
        return found[0]
    return [found[3 * n : 3 * n + 3] for n in range(blocks)]


def project_out(place, mine, got, weights, tiles=2):
    blocks, rows, half = mine.shape
    quarter = rows // 4
    tile = weights.shape[0] // tiles
    held = blocks * rows // 2

    def kernel(place_ref, mine_ref, got_ref, weight_ref, kept_ref, sent_ref, context):
        core, plane = place_ref[1], place_ref[2]

        @pl.when(pl.program_id(0) == 0)
        def _():
            for n, step in enumerate((0, 2, 1, 3)):
                begin = pl.ds(pl.multiple_of((plane ^ step) * quarter, quarter), quarter)
                for i in range(blocks):
                    here = pl.ds((n * blocks + i) * quarter, quarter)
                    lanes = pl.ds(pl.multiple_of(core * half, half), half)
                    context[here, lanes] = mine_ref[i, begin]
                    lanes = pl.ds(pl.multiple_of((1 - core) * half, half), half)
                    context[here, lanes] = got_ref[1 - i, begin]

        part = lax.dot_general(
            context[...],
            weight_ref[...],
            (((1,), (1,)), ((), ())),
            preferred_element_type=jnp.float32,
        )
        kept_ref[...] = part[:held]
        sent_ref[...] = part[held:].astype(jnp.bfloat16)

    def whole(a):
        return pl.BlockSpec(a.shape, lambda t: (0, 0, 0))

    return pl.pallas_call(
        kernel,
        grid=(tiles,),
        out_shape=[
            jax.ShapeDtypeStruct((held, tiles * tile), kind) for kind in (jnp.float32, jnp.bfloat16)
        ],
        in_specs=[
            smem_spec(),
            whole(mine),
            whole(got),
            pl.BlockSpec((tile, 2 * half), lambda t: (t, 0)),
        ],
        out_specs=[pl.BlockSpec((held, tile), lambda t: (0, t))] * 2,
        scratch_shapes=[pltpu.VMEM((2 * held, 2 * half), jnp.bfloat16)],
        compiler_params=pltpu.CompilerParams(vmem_limit_bytes=VMEM),
        cost_estimate=pl.CostEstimate(
            flops=2 * 2 * held * 2 * half * tile * tiles,
            bytes_accessed=2 * tile * tiles * 2 * half,
            transcendentals=0,
        ),
        name="project_out",
    )(place, mine, got, weights)


def add_up(groups):
    rows, width = groups[0][2].shape
    rows //= 2

    def kernel(*refs):
        own_ref, other_ref = refs[-2:]
        for n in range(len(groups)):
            kept_ref, first_ref, second_ref = refs[3 * n : 3 * n + 3]
            total = kept_ref[...] + first_ref[...].astype(jnp.float32)
            total = (total + second_ref[...].astype(jnp.float32)).astype(jnp.bfloat16)
            here = slice(n * width, (n + 1) * width)
            own_ref[:, here] = total[:rows]
            other_ref[:, here] = total[rows:]

    args = [a for group in groups for a in group]
    shape = jax.ShapeDtypeStruct((rows, len(groups) * width), jnp.bfloat16)
    return pl.pallas_call(
        kernel,
        grid=(1,),
        out_shape=(shape, shape),
        in_specs=[pl.BlockSpec((2 * rows, width), lambda t: (0, 0))] * len(args),
        out_specs=[pl.BlockSpec(shape.shape, lambda t: (0, 0))] * 2,
        compiler_params=pltpu.CompilerParams(vmem_limit_bytes=VMEM),
        cost_estimate=pl.CostEstimate(
            flops=4 * rows * shape.shape[1],
            bytes_accessed=20 * rows * shape.shape[1],
            transcendentals=0,
        ),
        name="add_up",
    )(*args)


def put_in_place(place, chips, mine, got, lasts):
    rows = mine.shape[0]
    early = len(chips) - len(lasts)
    shard = mine.shape[1] // early

    def kernel(place_ref, *refs):
        out_ref = refs[-1]
        for n, whose in enumerate(chips):
            for core_step in range(2):
                if n < early:
                    value = refs[core_step][:, n * shard : (n + 1) * shard]
                else:
                    first = 2 + 4 * (n - early) + 2 * core_step
                    near_ref, away_ref = refs[first : first + 2]
                    value = near_ref[...] + away_ref[:rows].astype(jnp.float32)
                at = chip_of(place_ref, whose, core_step) * 2 + (place_ref[1] ^ core_step)
                begin = pl.multiple_of(at * shard, shard)
                out_ref[:, pl.ds(begin, shard)] = value.astype(jnp.bfloat16)

    args = [mine, got] + [a for last in lasts for a in last]
    return pl.pallas_call(
        kernel,
        out_shape=jax.ShapeDtypeStruct((rows, 8 * shard), jnp.bfloat16),
        in_specs=[smem_spec()] + [vmem_spec()] * len(args),
        out_specs=vmem_spec(),
        compiler_params=pltpu.CompilerParams(vmem_limit_bytes=VMEM),
        cost_estimate=pl.CostEstimate(
            flops=0, bytes_accessed=4 * rows * 8 * shard, transcendentals=0
        ),
        name="put_in_place",
    )(place, *args)


def plane_shards(decoder_states, w_query, w_out_t, enc_keys, enc_values):
    block, plane = lax.axis_index("blk"), lax.axis_index("fsdp")
    core = block % 2
    place = jnp.stack([block // 2, core, plane]).astype(jnp.int32)
    shard, rows = w_query.shape[0], enc_keys.shape[0]

    def half_of(a, which):
        width = a.shape[1] // 2
        return lax.dynamic_slice_in_dim(a, which * width, width, 1)

    def whole_rows(a, got):
        return jnp.concatenate([half_of(a, core), got])

    def add_passed(sums, first):
        begin = sums[0].shape[0] // 2
        return (sums[0][begin:] + first[begin:].astype(jnp.float32)).astype(jnp.bfloat16)

    def totals(sums, first):
        held, passed = jnp.split(sums[0] + first.astype(jnp.float32), 2)
        own, other = jnp.split(held, 2)
        return own, other, passed.astype(jnp.bfloat16)

    states_1 = over_z(decoder_states, 1)
    states_2 = over_z(decoder_states, 2)
    states_3 = over_z(states_2, 1)
    others = over_core(decoder_states)
    others_1 = over_core(after(states_1, others))
    others_2 = over_core(after(states_2, others_1))
    others_3 = over_core(after(states_3, others_2))
    to_swap = jnp.concatenate([half_of(a, 1 - core) for a in (w_query, enc_keys, enc_values)])
    swapped = over_core(to_swap)
    weights = jnp.concatenate([half_of(w_query, core), swapped[:shard]])
    near_weights = cross(weights)
    side_weights = cross_back(weights)
    far_weights = cross_back(after(near_weights, near_weights, side_weights, states_1, states_2))
    queries = project_queries(place, [decoder_states, states_1, states_2, states_3, others, others_1, others_2, others_3], [(OWN, weights), (NEAR, near_weights), (SIDE, side_weights), (FAR, far_weights)])
    encoded = jnp.concatenate([whole_rows(enc_keys, swapped[shard:-rows]), whole_rows(enc_values, swapped[-rows:])], axis=1)
    near_encoded = cross(after(encoded, states_1))
    before = attend(after(queries, side_weights), [encoded, near_encoded])
    side_encoded = cross_back(after(encoded, states_2, others_1))
    far_encoded = cross_back(near_encoded)
    context = attend(queries, [side_encoded, far_encoded], before)
    context_got = over_core(context)
    sums_0 = project_out(place, context, context_got, w_out_t)
    first_0 = over_z(sums_0[1], 1)
    near_out = cross(after(w_out_t, context))
    passed_0 = add_passed(after(sums_0, context_got, near_out), first_0)
    side_out = cross_back(after(w_out_t, before))
    sums_1 = project_out(place, after(context, sums_0), context_got, side_out)
    first_1 = over_z(sums_1[1], 1)
    second_0 = over_z(after(passed_0, first_1), 2)
    passed_1 = add_passed(sums_1, first_1)
    second_1 = over_z(passed_1, 2)
    far_out = cross(side_out)
    sums_2 = project_out(place, after(context, sums_1), context_got, near_out)
    sums_3 = project_out(place, after(context, sums_2), context_got, far_out)
    most_added = add_up([(after(sums_0, sums_3)[0], first_0, second_0), (sums_1[0], first_1, second_1)])
    most_got = over_core(most_added[1])
    first_2 = over_z(after(sums_2, context_got, context)[1], 1)
    passed_2 = totals(after(sums_2, far_out), first_2)
    second_2 = over_z(passed_2[2], 2)
    got_2 = over_core(passed_2[1])
    third_2 = over_core(second_2[second_2.shape[0] // 2 :])
    first_3 = over_z(sums_3[1], 1)
    passed_3 = totals(sums_3, first_3)
    second_3 = over_z(passed_3[2], 2)
    got_3 = over_core(passed_3[1])
    third_3 = over_core(second_3[second_3.shape[0] // 2 :])
    return put_in_place(place, (OWN, SIDE, NEAR, FAR), most_added[0], most_got, [(passed_2[0], second_2, got_2, third_2), (passed_3[0], second_3, got_3, third_3)])


def solution(mesh):
    in_specs = (
        P("blk", "fsdp"),
        P("blk", "fsdp"),
        P("blk", "fsdp"),
        P("blk", "fsdp"),
        P("blk", "fsdp"),
    )
    out_specs = P(("blk", "fsdp"), None)
    by_planes = mesh.shape["blk"] == 8 and mesh.shape["fsdp"] == 4
    return jax.shard_map(
        plane_shards if by_planes else gathered_shards,
        mesh=mesh,
        in_specs=in_specs,
        out_specs=out_specs,
        check_vma=False,
    )
```

```python
import math

import jax
import jax.numpy as jnp
from jax import lax
from jax.experimental import pallas as pl
from jax.experimental.pallas import tpu as pltpu
from jax.sharding import PartitionSpec as P

HEAD_DIM = 64
PAIR = 2 * HEAD_DIM
PAIRS_AT_ONCE = 2
VMEM = 60 * 1024 * 1024


def absorb(fold_state, query_heads, key_rows, value_rows):
    running_top, running_sum, weighted = fold_state
    local_heads = query_heads.shape[1]
    key_heads = key_rows.reshape(key_rows.shape[0], local_heads, HEAD_DIM)
    value_heads = value_rows.reshape(value_rows.shape[0], local_heads, HEAD_DIM)
    scores = jnp.einsum(
        "qhd,khd->hqk", query_heads, key_heads, preferred_element_type=jnp.float32
    ) * (1.0 / math.sqrt(HEAD_DIM))
    new_top = jnp.max(scores, axis=2)
    rescale = jnp.exp(running_top - new_top)
    probability = jnp.exp(scores - new_top[:, :, None])
    running_sum = running_sum * rescale + jnp.sum(probability, axis=2)
    weighted = weighted * rescale[:, :, None] + jnp.einsum(
        "hqk,khd->hqd",
        probability.astype(jnp.bfloat16),
        value_heads,
        preferred_element_type=jnp.float32,
    )
    return (new_top, running_sum, weighted)


def gathered_shards(decoder_states, w_query, w_out_t, enc_keys, enc_values):
    query_full = lax.all_gather(w_query, "blk", axis=0, tiled=True)
    row_count = decoder_states.shape[0]
    columns = query_full.shape[1]
    local_heads = columns // HEAD_DIM
    queries = jnp.dot(
        lax.all_gather(decoder_states, "fsdp", axis=1, tiled=True),
        query_full,
        preferred_element_type=jnp.float32,
    ).astype(jnp.bfloat16)
    start_state = (
        jnp.full((local_heads, row_count), -jnp.inf, jnp.float32),
        jnp.zeros((local_heads, row_count), jnp.float32),
        jnp.zeros((local_heads, row_count, HEAD_DIM), jnp.float32),
    )
    query_heads = queries.reshape(row_count, local_heads, HEAD_DIM)
    final_state = absorb(
        start_state,
        query_heads,
        lax.all_gather(enc_keys, "blk", axis=0, tiled=True),
        lax.all_gather(enc_values, "blk", axis=0, tiled=True),
    )
    context = final_state[2] / final_state[1][:, :, None]
    context = jnp.transpose(context, (1, 0, 2)).reshape(row_count, columns).astype(jnp.bfloat16)
    out_full = lax.all_gather(w_out_t, "blk", axis=0, tiled=True)
    return lax.psum_scatter(
        lax.dot_general(
            context, out_full, (((1,), (1,)), ((), ())), preferred_element_type=jnp.float32
        ),
        "fsdp",
        scatter_dimension=0,
        tiled=True,
    ).astype(jnp.bfloat16)


CORE = [(b, b ^ 1) for b in range(8)]
CROSS = [(b, b ^ (2 if b % 2 == 0 else 4)) for b in range(8)]
CROSS_BACK = [(b, b ^ (4 if b % 2 == 0 else 2)) for b in range(8)]

def over_core(a):
    return lax.ppermute(a, "blk", CORE)


def cross(a):
    return lax.ppermute(a, "blk", CROSS)


def cross_back(a):
    return lax.ppermute(a, "blk", CROSS_BACK)


def over_z(a, step):
    return lax.ppermute(a, "fsdp", [(z, z ^ step) for z in range(4)])


def after(value, *earlier):
    return lax.optimization_barrier((value,) + earlier)[0]


OWN, NEAR, SIDE, FAR = (0, 0), (1, 2), (2, 1), (3, 3)


def chip_of(place_ref, whose, core_step=0):
    chip, core = place_ref[0], place_ref[1] ^ core_step
    even, odd = whose
    return chip ^ (even + core * (odd - even))


def any_spec():
    return pl.BlockSpec(memory_space=pl.ANY)


def smem_spec():
    return pl.BlockSpec(memory_space=pltpu.SMEM)


def vmem_spec():
    return pl.BlockSpec(memory_space=pltpu.VMEM)


def project_queries(place, states, weights):
    rows, depth = states[0].shape
    columns = weights[0][1].shape[1]
    shard = depth // 2

    def kernel(place_ref, *refs):
        state_refs = refs[: len(states)]
        weight_refs = refs[len(states) : len(states) + len(weights)]
        mine_ref, other_ref, state_s, weight_s, total, sems = refs[len(states) + len(weights) :]
        core, plane = place_ref[1], place_ref[2]
        chips = [chip_of(place_ref, whose) for whose, _ in weights]

        def copy_states(which, n):
            here = pl.ds(n // 4 * rows, rows)
            sem = sems.at[n // 4, plane ^ (n % 4)] if which is None else sems.at[n // 4, which]
            at = plane ^ (n % 4) if which is None else which
            return pltpu.make_async_copy(state_refs[n], state_s.at[at, here], sem)

        def copy_weights(n, part):
            begin = pl.multiple_of((core ^ part) * shard, shard)
            return pltpu.make_async_copy(
                weight_refs[n].at[pl.ds(part * shard, shard)],
                weight_s.at[chips[n], pl.ds(begin, shard)],
                sems.at[2 + part, n],
            )

        for n in range(4):
            copy_states(None, n).start()
            copy_states(None, n + 4).start()
            copy_weights(n, 0).start()
            copy_weights(n, 1).start()
        for n, chip_at in enumerate(chips):
            copy_states(chip_at, 0).wait()
            copy_states(chip_at, 4).wait()
            copy_weights(n, 0).wait()
            copy_weights(n, 1).wait()
            part = jnp.dot(state_s[chip_at], weight_s[chip_at], preferred_element_type=jnp.float32)
            total[...] = part if n == 0 else total[...] + part
        factor = 1.0 / math.sqrt(HEAD_DIM)
        for ref, first in ((mine_ref, 0), (other_ref, rows)):
            queries = total[first : first + rows].astype(jnp.bfloat16)
            ref[...] = (queries.astype(jnp.float32) * factor).astype(jnp.bfloat16)

    shape = jax.ShapeDtypeStruct((rows, columns), jnp.bfloat16)
    return pl.pallas_call(
        kernel,
        out_shape=(shape, shape),
        in_specs=[smem_spec()] + [any_spec()] * (len(states) + len(weights)),
        out_specs=(vmem_spec(), vmem_spec()),
        scratch_shapes=[
            pltpu.VMEM((4, 2 * rows, depth), jnp.bfloat16),
            pltpu.VMEM((4, depth, columns), jnp.bfloat16),
            pltpu.VMEM((2 * rows, columns), jnp.float32),
            pltpu.SemaphoreType.DMA((4, 4)),
        ],
        compiler_params=pltpu.CompilerParams(vmem_limit_bytes=VMEM),
        cost_estimate=pl.CostEstimate(
            flops=4 * rows * 4 * depth * columns,
            bytes_accessed=2 * 4 * depth * (2 * rows + columns),
            transcendentals=0,
        ),
        name="project_queries",
    )(place, *states, *[w[1] for w in weights])


def pair_part(queries, keys, values, tile=64):
    keys, values = jnp.concatenate(keys, axis=0), jnp.concatenate(values, axis=0)
    first = lax.broadcasted_iota(jnp.int32, (tile, PAIR), 1) < HEAD_DIM
    found = []
    for begin in range(0, queries.shape[0], tile):
        rows = queries[begin : begin + tile]
        masked = jnp.concatenate([jnp.where(first, rows, 0), jnp.where(first, 0, rows)], axis=0)
        scores = lax.dot_general(
            masked, keys, (((1,), (1,)), ((), ())), preferred_element_type=jnp.float32
        )
        top = scores.max(axis=1, keepdims=True)
        probability = jnp.exp(scores - top).astype(jnp.bfloat16)
        both = jnp.dot(probability, values, preferred_element_type=jnp.float32)
        top = jnp.broadcast_to(top, (2 * tile, PAIR))
        parts = both[:, :PAIR], both[:, PAIR:], top
        found.append([jnp.where(first, a[:tile], a[tile:]) for a in parts])
    return [jnp.concatenate(a, axis=0) for a in zip(*found)]


def attend(query_blocks, pieces, before=None, last=True):
    rows, columns = query_blocks[0].shape
    width = PAIRS_AT_ONCE * PAIR
    steps = columns // width
    blocks = len(query_blocks)
    last = last and before is not None
    held = [] if before is None else [a for block in before for a in block]
    outs = 1 if last else 3 * blocks

    def kernel(*refs):
        refs = list(refs)
        q_refs = [refs.pop(0) for _ in range(blocks)]
        k_refs = [refs.pop(0) for _ in pieces]
        v_refs = [refs.pop(0) for _ in pieces]
        held_refs = [refs.pop(0) for _ in held]
        out_refs = [refs.pop(0) for _ in range(outs)]
        for pair in range(PAIRS_AT_ONCE):
            at = slice(pair * PAIR, (pair + 1) * PAIR)
            ks = [r[:, at] for r in k_refs]
            ones = [jnp.ones((r.shape[0], PAIR), jnp.bfloat16) for r in v_refs]
            vs = [jnp.concatenate([r[:, at], one], axis=1) for r, one in zip(v_refs, ones)]
            for n in range(blocks):
                weighted, sums, tops = pair_part(q_refs[n][:, at], ks, vs)
                if held:
                    weighted_0, sums_0, tops_0 = (r[:, at] for r in held_refs[3 * n : 3 * n + 3])
                    top = jnp.maximum(tops, tops_0)
                    now, then = jnp.exp(tops - top), jnp.exp(tops_0 - top)
                    weighted = weighted * now + weighted_0 * then
                    sums = sums * now + sums_0 * then
                    tops = top
                if last:
                    out_refs[0][n, :, at] = (weighted / sums).astype(jnp.bfloat16)
                else:
                    for ref, a in zip(out_refs[3 * n : 3 * n + 3], (weighted, sums, tops)):
                        ref[:, at] = a

    def spec(a, skip=0):
        return pl.BlockSpec((a.shape[0], width), lambda p: (0, p + skip))

    args = list(query_blocks) + list(pieces) + list(pieces) + held
    in_specs = (
        [spec(a) for a in query_blocks]
        + [spec(a) for a in pieces]
        + [spec(a, steps) for a in pieces]
        + [spec(a) for a in held]
    )
    out_shape = [jax.ShapeDtypeStruct((rows, columns), jnp.float32)] * outs
    out_specs = [spec(a) for a in out_shape]
    if last:
        out_shape = [jax.ShapeDtypeStruct((blocks, rows, columns), jnp.bfloat16)]
        out_specs = [pl.BlockSpec((blocks, rows, width), lambda p: (0, 0, p))]
    total_keys = sum(a.shape[0] for a in pieces)
    found = pl.pallas_call(
        kernel,
        grid=(steps,),
        out_shape=out_shape,
        in_specs=in_specs,
        out_specs=out_specs,
        compiler_params=pltpu.CompilerParams(vmem_limit_bytes=VMEM),
        cost_estimate=pl.CostEstimate(
            flops=2 * 2 * blocks * rows * total_keys * columns * 4,
            bytes_accessed=sum(a.size * a.dtype.itemsize for a in args),
            transcendentals=blocks * rows * total_keys * (columns // HEAD_DIM),
        ),
        name=f"attend_{'last' if last else 'next' if held else 'first'}_{len(pieces)}",
    )(*args)
    if last:
        return found[0]
    return [found[3 * n : 3 * n + 3] for n in range(blocks)]


def project_out(place, mine, got, weights, tiles=2):
    blocks, rows, half = mine.shape
    quarter = rows // 4
    tile = weights.shape[0] // tiles
    held = blocks * rows // 2

    def kernel(place_ref, mine_ref, got_ref, weight_ref, kept_ref, sent_ref, context):
        core, plane = place_ref[1], place_ref[2]

        @pl.when(pl.program_id(0) == 0)
        def _():
            for n, step in enumerate((0, 2, 1, 3)):
                begin = pl.ds(pl.multiple_of((plane ^ step) * quarter, quarter), quarter)
                for i in range(blocks):
                    here = pl.ds((n * blocks + i) * quarter, quarter)
                    lanes = pl.ds(pl.multiple_of(core * half, half), half)
                    context[here, lanes] = mine_ref[i, begin]
                    lanes = pl.ds(pl.multiple_of((1 - core) * half, half), half)
                    context[here, lanes] = got_ref[1 - i, begin]

        part = lax.dot_general(
            context[...],
            weight_ref[...],
            (((1,), (1,)), ((), ())),
            preferred_element_type=jnp.float32,
        )
        kept_ref[...] = part[:held]
        sent_ref[...] = part[held:].astype(jnp.bfloat16)

    def whole(a):
        return pl.BlockSpec(a.shape, lambda t: (0, 0, 0))

    return pl.pallas_call(
        kernel,
        grid=(tiles,),
        out_shape=[
            jax.ShapeDtypeStruct((held, tiles * tile), kind) for kind in (jnp.float32, jnp.bfloat16)
        ],
        in_specs=[
            smem_spec(),
            whole(mine),
            whole(got),
            pl.BlockSpec((tile, 2 * half), lambda t: (t, 0)),
        ],
        out_specs=[pl.BlockSpec((held, tile), lambda t: (0, t))] * 2,
        scratch_shapes=[pltpu.VMEM((2 * held, 2 * half), jnp.bfloat16)],
        compiler_params=pltpu.CompilerParams(vmem_limit_bytes=VMEM),
        cost_estimate=pl.CostEstimate(
            flops=2 * 2 * held * 2 * half * tile * tiles,
            bytes_accessed=2 * tile * tiles * 2 * half,
            transcendentals=0,
        ),
        name="project_out",
    )(place, mine, got, weights)


def add_up(groups):
    rows, width = groups[0][2].shape
    rows //= 2

    def kernel(*refs):
        own_ref, other_ref = refs[-2:]
        for n in range(len(groups)):
            kept_ref, first_ref, second_ref = refs[3 * n : 3 * n + 3]
            total = kept_ref[...] + first_ref[...].astype(jnp.float32)
            total = (total + second_ref[...].astype(jnp.float32)).astype(jnp.bfloat16)
            here = slice(n * width, (n + 1) * width)
            own_ref[:, here] = total[:rows]
            other_ref[:, here] = total[rows:]

    args = [a for group in groups for a in group]
    shape = jax.ShapeDtypeStruct((rows, len(groups) * width), jnp.bfloat16)
    return pl.pallas_call(
        kernel,
        grid=(1,),
        out_shape=(shape, shape),
        in_specs=[pl.BlockSpec((2 * rows, width), lambda t: (0, 0))] * len(args),
        out_specs=[pl.BlockSpec(shape.shape, lambda t: (0, 0))] * 2,
        compiler_params=pltpu.CompilerParams(vmem_limit_bytes=VMEM),
        cost_estimate=pl.CostEstimate(
            flops=4 * rows * shape.shape[1],
            bytes_accessed=20 * rows * shape.shape[1],
            transcendentals=0,
        ),
        name="add_up",
    )(*args)


def put_in_place(place, chips, mine, got, lasts):
    rows = mine.shape[0]
    early = len(chips) - len(lasts)
    shard = mine.shape[1] // early

    def kernel(place_ref, *refs):
        out_ref = refs[-1]
        for n, whose in enumerate(chips):
            for core_step in range(2):
                if n < early:
                    value = refs[core_step][:, n * shard : (n + 1) * shard]
                else:
                    first = 2 + 4 * (n - early) + 2 * core_step
                    near_ref, away_ref = refs[first : first + 2]
                    value = near_ref[...] + away_ref[:rows].astype(jnp.float32)
                at = chip_of(place_ref, whose, core_step) * 2 + (place_ref[1] ^ core_step)
                begin = pl.multiple_of(at * shard, shard)
                out_ref[:, pl.ds(begin, shard)] = value.astype(jnp.bfloat16)

    args = [mine, got] + [a for last in lasts for a in last]
    return pl.pallas_call(
        kernel,
        out_shape=jax.ShapeDtypeStruct((rows, 8 * shard), jnp.bfloat16),
        in_specs=[smem_spec()] + [vmem_spec()] * len(args),
        out_specs=vmem_spec(),
        compiler_params=pltpu.CompilerParams(vmem_limit_bytes=VMEM),
        cost_estimate=pl.CostEstimate(
            flops=0, bytes_accessed=4 * rows * 8 * shard, transcendentals=0
        ),
        name="put_in_place",
    )(place, *args)


def plane_shards(decoder_states, w_query, w_out_t, enc_keys, enc_values):
    block, plane = lax.axis_index("blk"), lax.axis_index("fsdp")
    core = block % 2
    place = jnp.stack([block // 2, core, plane]).astype(jnp.int32)
    shard, rows = w_query.shape[0], enc_keys.shape[0]

    def half_of(a, which):
        width = a.shape[1] // 2
        return lax.dynamic_slice_in_dim(a, which * width, width, 1)

    def whole_rows(a, got):
        return jnp.concatenate([half_of(a, core), got])

    def add_passed(sums, first):
        begin = sums[0].shape[0] // 2
        return (sums[0][begin:] + first[begin:].astype(jnp.float32)).astype(jnp.bfloat16)

    def totals(sums, first):
        held, passed = jnp.split(sums[0] + first.astype(jnp.float32), 2)
        own, other = jnp.split(held, 2)
        return own, other, passed.astype(jnp.bfloat16)

    states_1 = over_z(decoder_states, 1)
    states_2 = over_z(decoder_states, 2)
    states_3 = over_z(states_2, 1)
    others = over_core(decoder_states)
    others_1 = over_core(after(states_1, others))
    others_2 = over_core(after(states_2, others_1))
    others_3 = over_core(after(states_3, others_2))
    to_swap = jnp.concatenate([half_of(a, 1 - core) for a in (w_query, enc_keys, enc_values)])
    swapped = over_core(to_swap)
    weights = jnp.concatenate([half_of(w_query, core), swapped[:shard]])
    near_weights = cross(weights)
    side_weights = cross_back(weights)
    far_weights = cross_back(after(near_weights, near_weights, side_weights, states_1, states_2))
    queries = project_queries(place, [decoder_states, states_1, states_2, states_3, others, others_1, others_2, others_3], [(OWN, weights), (NEAR, near_weights), (SIDE, side_weights), (FAR, far_weights)])
    encoded = jnp.concatenate([whole_rows(enc_keys, swapped[shard:-rows]), whole_rows(enc_values, swapped[-rows:])], axis=1)
    near_encoded = cross(after(encoded, states_1))
    before = attend(after(queries, side_weights), [encoded, near_encoded])
    side_encoded = cross_back(after(encoded, states_2, others_1))
    far_encoded = cross_back(near_encoded)
    context = attend(queries, [side_encoded, far_encoded], before)
    context_got = over_core(context)
    sums_0 = project_out(place, context, context_got, w_out_t)
    first_0 = over_z(sums_0[1], 1)
    near_out = cross(after(w_out_t, context))
    passed_0 = add_passed(after(sums_0, context_got, near_out), first_0)
    side_out = cross_back(after(w_out_t, before))
    sums_1 = project_out(place, after(context, sums_0), context_got, side_out)
    first_1 = over_z(sums_1[1], 1)
    second_0 = over_z(after(passed_0, first_1), 2)
    passed_1 = add_passed(sums_1, first_1)
    second_1 = over_z(passed_1, 2)
    far_out = cross(side_out)
    sums_2 = project_out(place, after(context, sums_1), context_got, near_out)
    sums_3 = project_out(place, after(context, sums_2), context_got, far_out)
    most_added = add_up([(after(sums_0, sums_3)[0], first_0, second_0), (sums_1[0], first_1, second_1)])
    most_got = over_core(most_added[1])
    first_2 = over_z(after(sums_2, context_got, context)[1], 1)
    passed_2 = totals(after(sums_2, far_out), first_2)
    second_2 = over_z(passed_2[2], 2)
    got_2 = over_core(passed_2[1])
    third_2 = over_core(second_2[second_2.shape[0] // 2 :])
    first_3 = over_z(sums_3[1], 1)
    passed_3 = totals(sums_3, first_3)
    second_3 = over_z(passed_3[2], 2)
    got_3 = over_core(passed_3[1])
    third_3 = over_core(second_3[second_3.shape[0] // 2 :])
    return put_in_place(place, (OWN, SIDE, NEAR, FAR), most_added[0], most_got, [(passed_2[0], second_2, got_2, third_2), (passed_3[0], second_3, got_3, third_3)])


def solution(mesh):
    in_specs = (
        P("blk", "fsdp"),
        P("blk", "fsdp"),
        P("blk", "fsdp"),
        P("blk", "fsdp"),
        P("blk", "fsdp"),
    )
    out_specs = P(("blk", "fsdp"), None)
    by_planes = mesh.shape["blk"] == 8 and mesh.shape["fsdp"] == 4
    return jax.shard_map(
        plane_shards if by_planes else gathered_shards,
        mesh=mesh,
        in_specs=in_specs,
        out_specs=out_specs,
        check_vma=False,
    )
```
